32 devices in a mesh: depth: 4 (over y, x), view: 8 (over z, core).
Axes of the slice: x: 2, y: 2, z: 4, core: 2. Of those that a mesh axis runs over, the one named last changes fastest.
Arguments:
- bricks: float32 [4, 8, 8, 64, 4096], P('depth', 'view'), may hold values from -6 to 6
- tile_holder: int32 [4, 8, 8], P('depth', 'view'), may hold values from -1 to 7, as said below
Outputs:
- image: float32 [4, 64, 4096], P(None, 'depth', 'view')
The draws below stay inside these ranges and needn't reach their ends.
Inputs may be any that keep to these rules, and one draw needn't show every extreme that they name: Renderer (d, v) finds brick column t in slot t of holder tile_holder[d, v, t]. For fixed d and t the holders that appear are distinct over v, and the holders named by one renderer are distinct; brick column 0 is never skipped.
All inputs are finite; a program needn't handle non-finite values.
Results may differ from the reference program's by a relative error of at most 0.0003.
Values sent between devices are 32-bit elements; how exact they have to be, the bound alone decides.
No kernel may reach another device: no remote copies, remote signals or barrier semaphores. Data moves between devices by JAX's collectives and lax.ppermute only.
A program may use at most 128 MiB of HBM per device.

```python
import jax
import jax.numpy as jnp
from jax import lax

BS = 64
TC_DEV = 8
STEPS = 48
N_DEPTH = 4
N_VIEW = 8


def draw_tile_holder(key, part):
    keys = jax.random.split(jax.random.fold_in(key, 17), 5)
    shuffle_keys = jax.random.split(keys[0], N_DEPTH)
    holder_perm = jax.vmap(lambda item: jax.random.permutation(item, N_VIEW))(shuffle_keys)
    shift_keys = jax.random.split(keys[1], N_DEPTH)
    shifts = jax.vmap(lambda item: jax.random.permutation(item, N_VIEW)[:TC_DEV])(shift_keys)
    views = jnp.arange(N_VIEW, dtype=jnp.int32)
    spots = (views[None, :, None] + shifts[:, None, :]) % N_VIEW
    holders = jax.vmap(lambda perm, where_at: perm[where_at])(holder_perm, spots)
    counts = jax.random.randint(keys[2], (N_DEPTH, N_VIEW), 1, TC_DEV + 1)
    lowest = jax.random.randint(keys[3], (N_DEPTH,), 0, N_VIEW)
    counts = jnp.where(views[None, :] == lowest[:, None], 1, counts)
    rank_keys = jax.random.split(keys[4], N_DEPTH * N_VIEW)
    ranks = jax.vmap(lambda item: jax.random.permutation(item, TC_DEV - 1))(rank_keys).reshape(N_DEPTH, N_VIEW, TC_DEV - 1)
    drawn_rest = ranks < counts[:, :, None] - 1
    drawn = jnp.concatenate([jnp.ones((N_DEPTH, N_VIEW, 1), dtype=bool), drawn_rest], axis=2)
    return jnp.where(drawn, holders, -1).astype(jnp.int32)


def steps_of(own_key, extent, cuts, smallest, largest):
    def one(position, blocks):
        steps = jax.random.uniform(jax.random.fold_in(jax.random.fold_in(own_key, 6), position), (blocks,), jnp.float32, smallest / len(cuts), largest / len(cuts))
        return jnp.repeat(jnp.exp(steps), extent[position] // blocks).reshape((-1,) + (1,) * (len(extent) - position - 1))

    level = one(*cuts[0])
    for cut in cuts[1:]:
        level = level * one(*cut)
    return level


def centred(stream_key, extent, spread, reach, cuts=(), kind=jnp.bfloat16):
    entries = jax.random.normal(stream_key, extent, jnp.float32) * spread
    if len(cuts) > 0:
        entries = steps_of(stream_key, extent, cuts, -0.22, 0.18) * entries
    return jnp.clip(entries, min=-reach, max=reach).astype(kind)


def setup_inputs(seed: int = 0) -> dict:
    arg_keys = jax.random.split(jax.random.key(seed), 3)
    bricks = centred(arg_keys[0], (N_DEPTH, N_VIEW, TC_DEV, BS, BS * BS), 1.0, 6.0, ((0, 4), (1, 8)), jnp.float32)
    tile_holder = draw_tile_holder(jax.random.fold_in(arg_keys[2], 71), 0)
    return dict(bricks=bricks, tile_holder=tile_holder)


DENSITY = 0.8
ISO_LEVEL = 1.0
SHARPEN = 1.5

def sample_table():
    spots = (jnp.arange(STEPS, dtype=jnp.float32) + 0.5) * (BS / STEPS) - 0.5
    spots = jnp.clip(spots, 0.0, BS - 1.0)
    voxels = jnp.arange(BS, dtype=jnp.float32)
    return jnp.maximum(0.0, 1.0 - jnp.abs(spots[:, None] - voxels[None, :])).astype(jnp.float32)

def prefix_table():
    steps_idx = jnp.arange(STEPS, dtype=jnp.int32)
    return (steps_idx[:, None] > steps_idx[None, :]).astype(jnp.float32)

def neighbor_diff(values):
    flat_idx = jnp.arange(BS * BS, dtype=jnp.int32)
    column = flat_idx % BS
    rowpos = flat_idx // BS
    right = jnp.where(column == BS - 1, values, jnp.roll(values, -1, axis=1))
    left = jnp.where(column == 0, values, jnp.roll(values, 1, axis=1))
    below = jnp.where(rowpos == BS - 1, values, jnp.roll(values, -BS, axis=1))
    above = jnp.where(rowpos == 0, values, jnp.roll(values, BS, axis=1))
    ahead = jnp.concatenate([values[1:], values[-1:]], axis=0)
    behind = jnp.concatenate([values[:1], values[:-1]], axis=0)
    return (right - left, below - above, ahead - behind)

def march_brick(brick, table, prefix):
    samples = jnp.dot(table, brick, precision=lax.Precision.HIGHEST)
    grad_x, grad_y, grad_z = neighbor_diff(samples)
    shade = 0.3 + 0.7 * jnp.abs(grad_z) / jnp.sqrt(grad_x * grad_x + grad_y * grad_y + grad_z * grad_z + 1.0)
    thickness = DENSITY / STEPS * jax.nn.sigmoid(4.0 * (samples - ISO_LEVEL))
    optical = jnp.dot(prefix, thickness, precision=lax.Precision.HIGHEST)
    weight = jnp.exp(-optical) * (1.0 - jnp.exp(-thickness))
    lit = weight * shade
    red_sum = lax.optimization_barrier(jnp.sum(lit * jax.nn.sigmoid(1.5 * samples), axis=0))
    green_sum = lax.optimization_barrier(jnp.sum(lit * jax.nn.sigmoid(-1.5 * samples), axis=0))
    blue_sum = lax.optimization_barrier(jnp.sum(lit * jax.nn.sigmoid(3.0 * (samples - 1.0)), axis=0))
    opacity = lax.optimization_barrier(jnp.sum(weight, axis=0))
    return jnp.stack([red_sum, green_sum, blue_sum, opacity], axis=0)

def composite_over(front, back, axis):
    front_alpha = lax.slice_in_dim(front, 3, 4, axis=axis)
    return front + (1.0 - front_alpha) * back

def sharpen_image(composite):
    padded = jnp.pad(composite, ((0, 0), (1, 1), (1, 1)))
    rows_done = 0.25 * padded[:, :-2] + 0.5 * padded[:, 1:-1] + 0.25 * padded[:, 2:]
    blurred = 0.25 * rows_done[:, :, :-2] + 0.5 * rows_done[:, :, 1:-1] + 0.25 * rows_done[:, :, 2:]
    return composite + SHARPEN * (composite - blurred)

def reference(bricks, tile_holder):
    table = sample_table()
    prefix = prefix_table()

    def render_slab(inputs):
        stored, holders = inputs
        flat = stored.reshape(N_VIEW * TC_DEV, BS, BS * BS)
        columns = jnp.arange(TC_DEV, dtype=jnp.int32)[None, :]
        indices = (jnp.clip(holders, 0, N_VIEW - 1) * TC_DEV + columns).reshape(-1).astype(jnp.int32)
        visible = (holders >= 0).astype(jnp.float32).reshape(-1)

        def one_tile(pair):
            index_one, shown = pair
            return march_brick(flat[index_one], table, prefix) * shown
        tiles = lax.map(one_tile, (indices, visible))
        tiles = tiles.reshape(N_VIEW * TC_DEV, 4, BS, BS)
        return tiles.transpose(1, 2, 0, 3).reshape(4, BS, N_VIEW * TC_DEV * BS)
    current = lax.map(render_slab, (bricks, tile_holder))
    while current.shape[0] > 1:
        paired = current.reshape((current.shape[0] // 2, 2) + current.shape[1:])
        current = composite_over(paired[:, 0], paired[:, 1], 1)
    return sharpen_image(current[0])
```

```python
import functools

import jax
import jax.numpy as jnp
from jax import lax
from jax.experimental import pallas as pl
from jax.experimental.pallas import tpu as pltpu
from jax.sharding import PartitionSpec as P

STEPS = 48
DENSITY = 0.8
SHARPEN = 1.5
LANES = 128
PHASES = 2


class Plan:
    def __init__(self, depths, views, columns, edge, area):
        self.depths, self.views, self.columns = depths, views, columns
        self.edge, self.area = edge, area
        self.pairs = area // LANES
        self.band = self.pairs // depths
        self.half = self.band // PHASES
        self.rows = 4 * self.half + 4
        self.blocks = -(-self.rows // 8)
        self.tiles = columns * depths
        self.slots = max(1, 8 // depths)
        self.subs = max(1, depths // 8)
        self.groups = columns // self.slots
        self.peers = depths * views
        self.zts = edge // 8


def roll(x, shift, axis=1):
    return pltpu.roll(x, shift % x.shape[axis], axis)


def lane_of(shape):
    return lax.broadcasted_iota(jnp.int32, shape, 1)


def march_group(plan, phase, load, top, bottom):
    half = plan.half
    scale = DENSITY / (2 * STEPS)
    lane = lane_of((8, LANES))
    low = lane < 64
    inside = (lane % 64 != 0).astype(jnp.float32)

    def three(zt, part):
        planes = [[load(zt, 4 * part + r, a) for a in range(half + 2)] for r in range(4)]
        first = [5.0 * p + q for p, q in zip(planes[0], planes[1])]
        second = [3.0 * (p + q) for p, q in zip(planes[1], planes[2])]
        third = [p + 5.0 * q for p, q in zip(planes[2], planes[3])]
        return [first, second, third]

    def step(index, behind, here, ahead, carry):
        body = here[1 : half + 1]
        turned = [roll(x, 64) for x in here]
        if phase == 0:
            turned[0] = jnp.where(top, body[0], turned[0])
        if phase == PHASES - 1:
            turned[-1] = jnp.where(bottom, body[-1], turned[-1])
        steps_y = [turned[i + 1] - turned[i] for i in range(half + 1)]
        out = []
        for a in range(half):
            total, trans, lit, red, blue = carry[a]
            x = body[a]
            grad_y = jnp.where(low, steps_y[a], steps_y[a + 1])
            diff = (x - roll(x, 1)) * inside
            grad_x = diff + roll(diff, -1)
            grad_z = ahead[a + 1] - behind[a + 1]
            norm = grad_x * grad_x + grad_y * grad_y + (grad_z * grad_z + 36.0)
            slope = jnp.abs(grad_z) * lax.rsqrt(norm)
            total = total + jnp.tanh(x * (1.0 / 3.0) - 2.0)
            later = jnp.exp(total * -scale - scale * (index + 1))
            part = (trans - later) * (slope + 3.0 / 7.0)
            out.append(
                (
                    total,
                    later,
                    lit + part,
                    red + part * jnp.tanh(x * 0.125),
                    blue + part * jnp.tanh(x * 0.25 - 1.5),
                )
            )
        return out

    zero = jnp.zeros((8, LANES), jnp.float32)
    carry = [(zero, zero + 1.0, zero, zero, zero)] * half
    window = []
    count = 0
    for zt in range(plan.zts):
        for part in range(2):
            for sample in three(zt, part):
                window.append(sample)
                if len(window) == 1:
                    window.append(sample)
                    window = [sample, sample]
                    continue
                if len(window) == 3:
                    carry = step(count, window[0], window[1], window[2], carry)
                    count += 1
                    window = window[1:]
    carry = step(count, window[0], window[1], window[1], carry)
    value = [[], [], [], []]
    for _, trans, lit, red, blue in carry:
        value[0].append(0.35 * (lit + red))
        value[1].append(0.35 * (lit - red))
        value[2].append(0.35 * (lit + blue))
        value[3].append(1.0 - trans)
    return value


def store_tiles(plan, phase, value, tiles_ref, base, first_slot):
    half = plan.half
    lane = lane_of((8, LANES))
    low = lane < 64
    rows = [value[c][a] for c in range(4) for a in range(half)]
    for c in (0, 2):
        if phase == 0:
            x, y = value[c][0], value[c + 1][0]
            rows.append(jnp.where(low, x, roll(y, 64)))
        else:
            x, y = value[c][-1], value[c + 1][-1]
            rows.append(jnp.where(low, roll(x, 64), y))
    first = jnp.zeros((8, LANES), jnp.float32)
    last = first
    for c in range(4):
        for a in range(half):
            spot = 4 * a + c
            first += roll(jnp.where(lane % 64 == 0, value[c][a], 0.0), spot)
            last += roll(jnp.where(lane % 64 == 63, value[c][a], 0.0), 4 * half + spot - 63)
    rim = jnp.where(first_slot, first, last)
    rows += [rim, rim]
    for i, row in enumerate(rows):
        start = ((i // 8) * plan.tiles + base) * 8 + i % 8
        tiles_ref[pl.ds(start, 8, 8), :] = row


def assemble(plan, phase, tiles_ref, route_ref, me_ref, out_ref):
    depths, views, half = plan.depths, plan.views, plan.half
    mine = me_ref[0]
    row = lax.broadcasted_iota(jnp.int32, (4, LANES), 0)
    zero = jnp.zeros((4, LANES), jnp.float32)

    def piece(slot, band, index):
        at = ((4 * index // 8) * plan.tiles + slot * depths + band) * 8 + 4 * index % 8
        return tiles_ref[pl.ds(at, 4), :]

    asked = [route_ref[mine * views + v, 0] for v in range(views)]
    for v in range(views):
        slot = jnp.maximum(asked[v], 0)
        right = left = None
        if v + 1 < views:
            right = jnp.where(asked[v + 1] == 0, 1.0, 0.0)
        if v > 0:
            left = jnp.where(asked[v - 1] == plan.columns - 1, 1.0, 0.0)

        def rim(band):
            total = zero
            if right is not None:
                total = total + right * piece(0, band, half)
            if left is not None:
                total = total + left * piece(plan.columns - 1, band, half)
            return total

        for band in range(depths):
            at = (band * views + v) * plan.rows
            for index in range(half):
                out_ref[pl.ds(at + 4 * index, 4), :] = piece(slot, band, index)
            near = band + 1 if phase == 0 else band - 1
            exists = 0 <= near < depths
            outer = piece(slot, near, half) if exists else zero
            corner = rim(near) if exists else zero
            tail = jnp.where(row < 2, outer, jnp.where(row == 2, rim(band), corner))
            out_ref[pl.ds(at + 4 * half, 4), :] = tail


def march_kernel(plan, phase, joined, *refs):
    if joined:
        route_ref, me_ref, x_ref, out_ref, tiles_ref, held, sems = refs
    else:
        x_ref, tiles_ref, held, sems = refs
    step = pl.program_id(0)
    half, depths = plan.half, plan.depths
    wide = min(depths, 8)

    def copies(group, parity):
        result = []
        for sub in range(plan.subs):
            for slot in range(plan.slots):
                for a in range(half + 2):
                    at = half * phase - 1 + a
                    move = -1 if at < 0 else (1 if at >= plan.band else 0)
                    at = at % plan.band
                    begin = sub * 8 + move
                    end = min(begin + wide, depths)
                    start = max(begin, 0)
                    source = x_ref.at[group * plan.slots + slot, :, pl.ds(start, end - start), at]
                    target = held.at[
                        parity, sub, :, a, pl.ds(slot * wide + start - begin, end - start)
                    ]
                    result.append(
                        pltpu.make_async_copy(source, target, sems.at[parity, len(result)])
                    )
        return result

    @pl.when(step == 0)
    def _():
        for copy in copies(0, 0):
            copy.start()

    @pl.when(step + 1 < plan.groups)
    def _():
        for copy in copies(step + 1, (step + 1) % 2):
            copy.start()

    for copy in copies(step, step % 2):
        copy.wait()

    size = plan.zts * (half + 2) * 64
    flat = held.reshape(2 * plan.subs * size, LANES)
    sub_row = lax.broadcasted_iota(jnp.int32, (8, LANES), 0)
    for sub in range(plan.subs):
        origin = ((step % 2) * plan.subs + sub) * size

        def load(zt, r, a):
            return flat[pl.ds(origin + (zt * (half + 2) + a) * 64 + r, 8, 8), :]

        top = sub_row % wide == 0 if sub == 0 else None
        bottom = sub_row % wide == wide - 1 if sub == plan.subs - 1 else None
        never = sub_row < 0
        value = march_group(
            plan, phase, load, never if top is None else top, never if bottom is None else bottom
        )
        first_slot = step * plan.slots + sub_row // wide == 0
        base = step * plan.slots * depths + 8 * sub
        store_tiles(plan, phase, value, tiles_ref, base, first_slot)

    if joined:

        @pl.when(step == plan.groups - 1)
        def _():
            assemble(plan, phase, tiles_ref, route_ref, me_ref, out_ref)


SMEM = pl.BlockSpec(memory_space=pltpu.SMEM)


def march(plan, phase, bricks, route=None):
    joined = route is not None
    tiles = (plan.blocks * plan.tiles * 8, LANES)
    shape = (plan.peers * plan.rows, LANES) if joined else tiles
    copies = plan.subs * plan.slots * (plan.half + 2)
    held = (2, plan.subs, plan.zts, plan.half + 2, 8, 8, LANES)
    scratch = [pltpu.VMEM(tiles, jnp.float32)] if joined else []
    pixels = plan.columns * plan.area // PHASES
    return pl.pallas_call(
        functools.partial(march_kernel, plan, phase, joined),
        grid=(plan.groups,),
        in_specs=([SMEM, SMEM] if joined else []) + [pl.BlockSpec(memory_space=pl.ANY)],
        out_specs=pl.BlockSpec(shape, lambda i: (0, 0)),
        out_shape=jax.ShapeDtypeStruct(shape, jnp.float32),
        scratch_shapes=scratch
        + [pltpu.VMEM(held, jnp.float32), pltpu.SemaphoreType.DMA((2, copies))],
        cost_estimate=pl.CostEstimate(
            flops=40 * STEPS * pixels, bytes_accessed=6 * plan.edge * pixels, transcendentals=5 * STEPS * pixels
        ),
        name=f"march_{phase}",
    )(*(route if joined else ()), bricks)


def assemble_kernel(plan, phase, route_ref, me_ref, tiles_ref, out_ref):
    assemble(plan, phase, tiles_ref, route_ref, me_ref, out_ref)


def message(plan, phase, tiles, route):
    return pl.pallas_call(
        functools.partial(assemble_kernel, plan, phase),
        in_specs=[SMEM, SMEM, pl.BlockSpec(memory_space=pltpu.VMEM)],
        out_specs=pl.BlockSpec(memory_space=pltpu.VMEM),
        out_shape=jax.ShapeDtypeStruct((plan.peers * plan.rows, LANES), jnp.float32),
        name=f"message_{phase}",
    )(*route, tiles)


def finish_kernel(plan, route_ref, me_ref, near_ref, far_ref, out_ref, image):
    depths, views, half, band = plan.depths, plan.views, plan.half, plan.band
    columns = plan.columns
    lane = lane_of((1, LANES))
    low = lane < 64
    view = me_ref[1]
    sources = (near_ref, far_ref)
    side = 4 * half

    def over(front, alpha, back):
        return front if back is None else front + (1.0 - alpha) * back

    bodies, outers = [], []
    for t in range(columns):
        body, outer = [], []
        for ref in sources:
            acc, rim = [None] * 4, [None] * 2
            for d in reversed(range(depths)):
                holder = route_ref[d * views + view, 1 + t]
                shown = jnp.where(holder >= 0, 1.0, 0.0)
                at = (d * views + jnp.maximum(holder, 0)) * plan.rows
                front = [ref[pl.ds(at + c * half, half), :] * shown for c in range(4)]
                acc = [over(f, front[3], b) for f, b in zip(front, acc)]
                front = [ref[pl.ds(at + 4 * half + i, 1), :] * shown for i in range(2)]
                alpha = jnp.where(low, roll(front[1], 64), front[1])
                rim = [over(f, alpha, b) for f, b in zip(front, rim)]
            body.append(acc)
            outer.append(rim)
        bodies.append([jnp.concatenate([body[0][c], body[1][c]], axis=0) for c in range(4)])
        outers.append(outer)

    sides = []
    lane2 = lane_of((2, LANES))
    for ref in sources:
        acc = None
        for d in reversed(range(depths)):
            front = None
            for h in range(views):
                piece = ref[pl.ds((d * views + h) * plan.rows + 4 * half + 2, 2), :]
                front = piece if front is None else front + piece
            alpha = front
            for c in range(3):
                alpha = jnp.where(lane2 % 4 == c, roll(front, c - 3), alpha)
            acc = over(front, alpha, acc)
        sides.append(acc)

    count = 2 * band
    wide = lane_of((band, LANES))
    low_band = wide < 64
    number = lax.broadcasted_iota(jnp.int32, (band, LANES), 0) % half
    final = columns // 2 + 1
    spread = jnp.concatenate(
        [jnp.broadcast_to(s[0:1], (half, LANES)) for s in sides], axis=0
    )
    for c in range(4):
        for u in range(columns // 2):
            x, y = bodies[2 * u][c], bodies[2 * u + 1][c]
            image[c, u + 1, pl.ds(8, band, 2), :] = jnp.where(low_band, x, roll(y, 64))
            image[c, u + 1, pl.ds(9, band, 2), :] = jnp.where(low_band, roll(x, 64), y)
            for source, at in ((0, 8 + count), (1, 7)):
                x, y = outers[2 * u][source][c // 2], outers[2 * u + 1][source][c // 2]
                if c % 2 == 0:
                    y = roll(y, 64)
                else:
                    x = roll(x, 64)
                image[c, u + 1, pl.ds(at, 1), :] = jnp.where(low, x, y)
        for base, tile, spot in ((0, final, 0), (side, 0, LANES - 1)):
            for odd in range(2):
                here = wide == base + 64 * odd + 4 * number + c
                column = jnp.sum(jnp.where(here, spread, 0.0), axis=1, keepdims=True)
                image[c, tile, pl.ds(8 + odd, band, 2), :] = jnp.where(wide == spot, column, 0.0)
            for source, at, where in (
                (0, 8 + count, base + c),
                (1, 7, 64 + base + 4 * (half - 1) + c),
            ):
                corner = jnp.sum(
                    jnp.where(lane == where, sides[source][1:2], 0.0), axis=1, keepdims=True
                )
                image[c, tile, pl.ds(at, 1), :] = jnp.where(lane == spot, corner, 0.0)

    full = lane_of((count, LANES))
    for c in range(4):
        middle = [image[c, k, pl.ds(8, count), :] for k in range(final + 1)]
        smooth = [
            0.25 * image[c, k, pl.ds(7, count), :]
            + 0.5 * middle[k]
            + 0.25 * image[c, k, pl.ds(9, count), :]
            for k in range(final + 1)
        ]
        later = [roll(x, 1) for x in smooth]
        sooner = [roll(x, -1) for x in smooth]
        for k in range(1, final):
            left = jnp.where(full == 0, later[k - 1], later[k])
            right = jnp.where(full == LANES - 1, sooner[k + 1], sooner[k])
            blurred = 0.25 * left + 0.5 * smooth[k] + 0.25 * right
            out_ref[c, :, pl.ds((k - 1) * LANES, LANES)] = middle[k] + SHARPEN * (
                middle[k] - blurred
            )


def finish(plan, near, far, route):
    count = 2 * plan.band
    return pl.pallas_call(
        functools.partial(finish_kernel, plan),
        in_specs=[SMEM, SMEM] + [pl.BlockSpec(memory_space=pltpu.VMEM)] * 2,
        out_specs=pl.BlockSpec(memory_space=pltpu.VMEM),
        out_shape=jax.ShapeDtypeStruct((4, count, plan.columns * 64), jnp.float32),
        scratch_shapes=[
            pltpu.VMEM((4, plan.columns // 2 + 2, count + 16, LANES), jnp.float32)
        ],
        name="finish",
    )(*route, near, far)


def exchange(plan, messages):
    cut = messages.reshape(plan.peers, plan.rows // 4, 4, LANES)
    moved = lax.all_to_all(cut, ("depth", "view"), split_axis=0, concat_axis=0, tiled=True)
    return moved.reshape(plan.peers * plan.rows, LANES)


def body(bricks, tile_holder):
    depths, views = lax.axis_size("depth"), lax.axis_size("view")
    columns, edge, area = bricks.shape[2:]
    plan = Plan(depths, views, columns, edge, area)
    holders = tile_holder[0, 0]
    matches = holders[:, None] == jnp.arange(views, dtype=jnp.int32)[None, :]
    slots = jnp.arange(columns, dtype=jnp.int32)[:, None]
    wanted = jnp.max(jnp.where(matches, slots, -1), axis=0)
    request = jnp.concatenate(
        [wanted[:, None], jnp.broadcast_to(holders[None, :], (views, columns))], axis=1
    )
    request = jnp.broadcast_to(request[None], (depths, views, columns + 1))
    request = request.reshape(plan.peers, columns + 1)
    route = lax.all_to_all(request, ("depth", "view"), split_axis=0, concat_axis=0, tiled=True)
    me = jnp.stack([lax.axis_index("depth"), lax.axis_index("view")]).astype(jnp.int32)
    route = (route, me)
    stored = bricks[0, 0].reshape(columns, plan.zts, 8, plan.pairs, LANES).transpose(0, 1, 3, 2, 4)
    stored = stored.reshape(columns, plan.zts, depths, plan.band, 8, LANES)
    tiles = march(plan, 0, stored)
    near = exchange(plan, message(plan, 0, tiles, route))
    far = exchange(plan, march(plan, 1, stored, route))
    return finish(plan, near, far, route)


def solution(mesh):
    in_specs = (P("depth", "view", None, None, None), P("depth", "view", None))
    out_specs = P(None, "depth", "view")
    return jax.shard_map(body, mesh=mesh, in_specs=in_specs, out_specs=out_specs, check_vma=False)
```

```python
import functools

import jax
import jax.numpy as jnp
from jax import lax
from jax.experimental import pallas as pl
from jax.experimental.pallas import tpu as pltpu
from jax.sharding import PartitionSpec as P

STEPS = 48
DENSITY = 0.8
SHARPEN = 1.5
LANES = 128
EARLY = 2
MARCH_BYTES = 57 * 1024 * 1024
FINISH_BYTES = 16 * 1024 * 1024


class Plan:
    def __init__(self, depths, views, columns, edge, area):
        self.depths, self.views, self.columns = depths, views, columns
        self.pairs = area // LANES
        self.band = self.pairs // depths
        self.rows = 4 * self.band + 6
        self.peers = depths * views
        self.zts = edge // 8
        self.regs = self.pairs // 8
        self.run = min(self.regs, self.band)
        self.tops = [a for a in range(self.regs) if a % self.band == 0]
        self.bottoms = [a for a in range(self.regs) if (a + 1) % self.run == 0][-len(self.tops) :]
        self.blocks = 3 if len(self.tops) == 1 else 4

    def run_of(self, band):
        pair = band * self.band
        return pair // self.regs, pair % self.regs


def roll(x, shift, axis=1):
    return pltpu.roll(x, shift % x.shape[axis], axis)


def lane_of(shape):
    return lax.broadcasted_iota(jnp.int32, shape, 1)


def march_tile(plan, load):
    scale = DENSITY / (2 * STEPS)
    regs = plan.regs
    lane = lane_of((8, LANES))
    row = lax.broadcasted_iota(jnp.int32, (8, LANES), 0)
    low = lane < 64
    inside = (lane % 64 != 0).astype(jnp.float32)
    top, bottom = row == 0, row == 7
    third = 1.0 / 3.0

    def three(zt, part):
        planes = [[load(zt, 4 * part + r, a) for a in range(regs)] for r in range(4)]
        first = [(5.0 * third) * p + third * q for p, q in zip(planes[0], planes[1])]
        second = [p + q for p, q in zip(planes[1], planes[2])]
        last = [third * p + (5.0 * third) * q for p, q in zip(planes[2], planes[3])]
        return [first, second, last]

    def step(index, behind, here, ahead, carry):
        turned = [roll(x, 64) for x in here]
        after = jnp.where(bottom, here[-1], roll(turned[0], -1, 0))
        steps_y = [y - x for x, y in zip(turned, turned[1:] + [after])]
        before = jnp.where(top, turned[0] - here[0], roll(steps_y[-1], 1, 0))
        steps_y = [before] + steps_y
        out = []
        for a in range(regs):
            total, trans, lit, red, blue = carry[a]
            x = here[a]
            grad_y = jnp.where(low, steps_y[a], steps_y[a + 1])
            diff = (x - roll(x, 1)) * inside
            grad_x = diff + roll(diff, -1)
            grad_z = ahead[a] - behind[a]
            norm = grad_x * grad_x + grad_y * grad_y + (grad_z * grad_z + 4.0)
            slope = jnp.abs(grad_z) * lax.rsqrt(norm)
            total = total + jnp.tanh(x - 2.0)
            later = jnp.exp(total * -scale - scale * (index + 1))
            part = (trans - later) * (slope + 3.0 / 7.0)
            red = red + part * jnp.tanh(x * 0.375)
            blue = blue + part * jnp.tanh(x * 0.75 - 1.5)
            out.append((total, later, lit + part, red, blue))
        return out

    zero = jnp.zeros((8, LANES), jnp.float32)
    carry = [(zero, zero + 1.0, zero, zero, zero)] * regs
    samples = [x for zt in range(plan.zts) for part in range(2) for x in three(zt, part)]
    padded = samples[:1] + samples + samples[-1:]
    for index in range(STEPS):
        carry = step(index, *padded[index : index + 3], carry)
    value = [[], [], [], []]
    for _, trans, lit, red, blue in carry:
        value[0].append(0.35 * (lit + red))
        value[1].append(0.35 * (lit - red))
        value[2].append(0.35 * (lit + blue))
        value[3].append(1.0 - trans)
    return value


def store_tile(plan, value, tiles_ref, slot, first_slot):
    regs = plan.regs
    lane = lane_of((8, LANES))
    low = lane < 64
    rows = [(c // 2, c % 2 * regs + a, value[c][a]) for c in range(4) for a in range(regs)]
    spot = 0
    for a in plan.tops:
        for c in (0, 2):
            edge = jnp.where(low, value[c][a], roll(value[c + 1][a], 64))
            rows.append((2 + spot // 8, spot % 8, edge))
            spot += 1
    for a in plan.bottoms:
        for c in (0, 2):
            edge = jnp.where(low, roll(value[c][a], 64), value[c + 1][a])
            rows.append((2 + spot // 8, spot % 8, edge))
            spot += 1
    first = last = jnp.zeros((8, LANES), jnp.float32)
    for c in range(4):
        for a in range(regs):
            at = 4 * a + c
            first += roll(jnp.where(lane % 64 == 0, value[c][a], 0.0), at)
            last += roll(jnp.where(lane % 64 == 63, value[c][a], 0.0), 4 * regs + at - 63)
    rows.append((2 + spot // 8, spot % 8, jnp.where(first_slot, first, last)))
    for block, at, row in rows:
        tiles_ref[block, pl.ds(slot * 64 + at, 8, 8), :] = row


def assemble(plan, tiles_ref, route_ref, out_ref):
    depths, views, columns = plan.depths, plan.views, plan.columns
    regs, run, band_pairs = plan.regs, plan.run, plan.band
    mine = route_ref[0, columns]
    depth, view = mine // views, mine % views
    lane = lane_of((1, LANES))
    zero = jnp.zeros((1, LANES), jnp.float32)
    rim_at = 2 * len(plan.tops) + 2 * len(plan.bottoms)

    def rows_of(block, slot, sublane, at, count):
        return tiles_ref[block, pl.ds(slot * 64 + sublane * 8 + at, count), :]

    asked = []
    for v in range(views):
        found = jnp.int32(-1)
        for t in range(columns):
            found = jnp.where(route_ref[depth * views + v, t] == view, t, found)
        asked.append(found)

    def rim(slot, sublane):
        return rows_of(2 + rim_at // 8, slot, sublane, rim_at % 8, 1)

    def above_of(band):
        sublane, a = plan.run_of(band)
        return (sublane, a - 1) if a > 0 else (sublane - 1, regs - 1)

    def below_of(band):
        sublane, a = plan.run_of(band)
        sublane, a = sublane + (a + band_pairs) // regs, (a + band_pairs) % regs
        return sublane, a

    own, corner = {}, {}
    for slot in (0, columns - 1):
        for band in range(depths):
            sublane, a = plan.run_of(band)
            total = zero
            for i in range(band_pairs // run):
                total = total + roll(rim(slot, sublane + i), 8 * regs * i - 4 * a)
            own[slot, band] = total
            total = zero
            if band > 0:
                sublane, a = above_of(band)
                moved = roll(rim(slot, sublane), 4 * (regs - 1 - a))
                keep = (lane % (4 * regs) >= 4 * (regs - 1)) & (lane >= 64)
                total = total + jnp.where(keep, moved, 0.0)
            if band < depths - 1:
                sublane, a = below_of(band)
                moved = roll(rim(slot, sublane), -4 * a)
                keep = (lane % (4 * regs) < 4) & (lane < 64)
                total = total + jnp.where(keep, moved, 0.0)
            corner[slot, band] = total

    for v in range(views):
        slot = jnp.maximum(asked[v], 0)
        sides = []
        if v + 1 < views:
            sides.append((0, jnp.where(asked[v + 1] == 0, 1.0, 0.0)))
        if v > 0:
            sides.append((columns - 1, jnp.where(asked[v - 1] == columns - 1, 1.0, 0.0)))
        for band in range(depths):
            at = (band * views + v) * plan.rows
            first, a = plan.run_of(band)
            for c in range(4):
                for i in range(band_pairs // run):
                    start = at + c * band_pairs + i * run
                    out_ref[pl.ds(start, run), :] = rows_of(
                        c // 2, slot, first + i, c % 2 * regs + a, run
                    )
            at += 4 * band_pairs
            above = below = jnp.zeros((2, LANES), jnp.float32)
            if band > 0:
                sublane, a = above_of(band)
                place = 2 * len(plan.tops) + 2 * plan.bottoms.index(a)
                above = rows_of(2 + place // 8, slot, sublane, place % 8, 2)
            if band < depths - 1:
                sublane, a = below_of(band)
                place = 2 * plan.tops.index(a)
                below = rows_of(2 + place // 8, slot, sublane, place % 8, 2)
            out_ref[pl.ds(at, 2), :] = above
            out_ref[pl.ds(at + 2, 2), :] = below
            out_ref[pl.ds(at + 4, 1), :] = sum(own[s, band] * f for s, f in sides) + zero
            out_ref[pl.ds(at + 5, 1), :] = sum(corner[s, band] * f for s, f in sides) + zero


def march_planes(plan, planes, tiles_ref, slot, first_slot):
    flat = [ref.reshape(plan.zts * 64, LANES) for ref in planes]

    def load(zt, r, a):
        return flat[a][pl.ds(zt * 64 + r, 8, 8), :]

    store_tile(plan, march_tile(plan, load), tiles_ref, slot, first_slot)


def early_kernel(plan, *refs):
    planes, tiles_ref = refs[:-1], refs[-1]
    step = pl.program_id(0)
    march_planes(plan, planes, tiles_ref, step, step == 0)


def late_kernel(plan, early, *refs):
    route_ref, early_ref = refs[:2]
    planes, (out_ref, tiles_ref, sem) = refs[2:-3], refs[-3:]
    step = pl.program_id(0)
    copy = pltpu.make_async_copy(early_ref, tiles_ref.at[:, pl.ds(0, early * 64)], sem)

    @pl.when(step == 0)
    def _():
        copy.start()

    march_planes(plan, planes, tiles_ref, step + early, step + early == 0)

    @pl.when(step == plan.columns - early - 1)
    def _():
        copy.wait()
        assemble(plan, tiles_ref, route_ref, out_ref)


SMEM = pl.BlockSpec(memory_space=pltpu.SMEM)
PARAMS = pltpu.CompilerParams(vmem_limit_bytes=MARCH_BYTES)


def plane_specs(plan, start):
    shape = (1, plan.zts, 8, 1, 8, LANES)

    def spec(a):
        return pl.BlockSpec(shape, lambda i: (start + i, 0, 0, a, 0, 0))

    return [spec(a) for a in range(plan.regs)]


def cost(plan, count):
    samples = count * plan.pairs * LANES * STEPS
    return pl.CostEstimate(
        flops=40 * samples, bytes_accessed=6 * samples, transcendentals=5 * samples
    )


def march_early(plan, stored):
    tiles = (plan.blocks, EARLY * 64, LANES)
    return pl.pallas_call(
        functools.partial(early_kernel, plan),
        grid=(EARLY,),
        in_specs=plane_specs(plan, 0),
        out_specs=pl.BlockSpec(tiles, lambda i: (0, 0, 0)),
        out_shape=jax.ShapeDtypeStruct(tiles, jnp.float32),
        cost_estimate=cost(plan, EARLY),
        compiler_params=PARAMS,
        name="march_early",
    )(*[stored] * plan.regs)


def march_late(plan, stored, early, route):
    shape = (plan.peers * plan.rows, LANES)
    return pl.pallas_call(
        functools.partial(late_kernel, plan, EARLY),
        grid=(plan.columns - EARLY,),
        in_specs=[SMEM, pl.BlockSpec(memory_space=pl.ANY)] + plane_specs(plan, EARLY),
        out_specs=pl.BlockSpec(shape, lambda i: (0, 0)),
        out_shape=jax.ShapeDtypeStruct(shape, jnp.float32),
        scratch_shapes=[
            pltpu.VMEM((plan.blocks, plan.columns * 64, LANES), jnp.float32),
            pltpu.SemaphoreType.DMA(()),
        ],
        cost_estimate=cost(plan, plan.columns - EARLY),
        compiler_params=PARAMS,
        name="march_late",
    )(route, early, *[stored] * plan.regs)


def finish_kernel(plan, route_ref, source, out_ref, image):
    depths, views, band, columns = plan.depths, plan.views, plan.band, plan.columns
    regs = plan.regs
    lane = lane_of((1, LANES))
    low = lane < 64
    view = route_ref[0, columns] % views

    def over(front, alpha, back):
        return front if back is None else front + (1.0 - alpha) * back

    bodies, outers = [], []
    for t in range(columns):
        acc, rims = [None] * 4, [[None] * 2, [None] * 2]
        for d in reversed(range(depths)):
            holder = route_ref[d * views + view, t]
            shown = jnp.where(holder >= 0, 1.0, 0.0)
            at = (d * views + jnp.maximum(holder, 0)) * plan.rows
            front = [source[pl.ds(at + c * band, band), :] * shown for c in range(4)]
            acc = [over(f, front[3], b) for f, b in zip(front, acc)]
            for side in range(2):
                place = at + 4 * band + 2 * side
                front = [source[pl.ds(place + i, 1), :] * shown for i in range(2)]
                alpha = jnp.where(low, roll(front[1], 64), front[1])
                rims[side] = [over(f, alpha, b) for f, b in zip(front, rims[side])]
        bodies.append(acc)
        outers.append(rims)

    sides = None
    lane2 = lane_of((2, LANES))
    for d in reversed(range(depths)):
        front = None
        for h in range(views):
            piece = source[pl.ds((d * views + h) * plan.rows + 4 * band + 4, 2), :]
            front = piece if front is None else front + piece
        alpha = front
        for c in range(3):
            alpha = jnp.where(lane2 % 4 == c, roll(front, c - 3), alpha)
        sides = over(front, alpha, sides)

    count = 2 * band
    wide = lane_of((band, LANES))
    low_band = wide < 64
    number = lax.broadcasted_iota(jnp.int32, (band, LANES), 0)
    number = 8 * regs * (number // regs) + 4 * (number % regs)
    final = columns // 2 + 1
    spread = jnp.broadcast_to(sides[0:1], (band, LANES))
    for c in range(4):
        for u in range(columns // 2):
            x, y = bodies[2 * u][c], bodies[2 * u + 1][c]
            image[c, u + 1, pl.ds(8, band, 2), :] = jnp.where(low_band, x, roll(y, 64))
            image[c, u + 1, pl.ds(9, band, 2), :] = jnp.where(low_band, roll(x, 64), y)
            for side, at in ((0, 7), (1, 8 + count)):
                x, y = outers[2 * u][side][c // 2], outers[2 * u + 1][side][c // 2]
                if c % 2 == 0:
                    y = roll(y, 64)
                else:
                    x = roll(x, 64)
                image[c, u + 1, pl.ds(at, 1), :] = jnp.where(low, x, y)
        for base, tile, spot in ((0, final, 0), (4 * regs, 0, LANES - 1)):
            for odd in range(2):
                here = wide == base + 64 * odd + number + c
                column = jnp.sum(jnp.where(here, spread, 0.0), axis=1, keepdims=True)
                image[c, tile, pl.ds(8 + odd, band, 2), :] = jnp.where(wide == spot, column, 0.0)
            for at, place in ((7, 64 + base + 4 * (regs - 1) + c), (8 + count, base + c)):
                pixel = jnp.where(lane == place, sides[1:2], 0.0)
                pixel = jnp.sum(pixel, axis=1, keepdims=True)
                image[c, tile, pl.ds(at, 1), :] = jnp.where(lane == spot, pixel, 0.0)

    full = lane_of((count, LANES))
    for c in range(4):
        middle = [image[c, k, pl.ds(8, count), :] for k in range(final + 1)]
        smooth = [
            0.25 * image[c, k, pl.ds(7, count), :]
            + 0.5 * middle[k]
            + 0.25 * image[c, k, pl.ds(9, count), :]
            for k in range(final + 1)
        ]
        later = [roll(x, 1) for x in smooth]
        sooner = [roll(x, -1) for x in smooth]
        for k in range(1, final):
            left = jnp.where(full == 0, later[k - 1], later[k])
            right = jnp.where(full == LANES - 1, sooner[k + 1], sooner[k])
            blurred = 0.25 * left + 0.5 * smooth[k] + 0.25 * right
            out_ref[c, :, pl.ds((k - 1) * LANES, LANES)] = middle[k] + SHARPEN * (
                middle[k] - blurred
            )


def finish(plan, arrived, route):
    count = 2 * plan.band
    return pl.pallas_call(
        functools.partial(finish_kernel, plan),
        in_specs=[SMEM, pl.BlockSpec(memory_space=pltpu.VMEM)],
        out_specs=pl.BlockSpec(memory_space=pltpu.VMEM),
        out_shape=jax.ShapeDtypeStruct((4, count, plan.columns * 64), jnp.float32),
        scratch_shapes=[
            pltpu.VMEM((4, plan.columns // 2 + 2, count + 16, LANES), jnp.float32)
        ],
        compiler_params=pltpu.CompilerParams(vmem_limit_bytes=FINISH_BYTES),
        name="finish",
    )(route, arrived)


def exchange(plan, messages):
    cut = messages.reshape(plan.peers, plan.rows // 2, 2, LANES)
    moved = lax.all_to_all(cut, ("depth", "view"), split_axis=0, concat_axis=0, tiled=True)
    return moved.reshape(plan.peers * plan.rows, LANES)


def body(bricks, tile_holder):
    depths, views = lax.axis_size("depth"), lax.axis_size("view")
    columns, edge, area = bricks.shape[2:]
    plan = Plan(depths, views, columns, edge, area)
    number = jnp.arange(plan.peers, dtype=jnp.int32)[:, None, None]
    place = jnp.arange(columns + 1, dtype=jnp.int32)[None, None, :]
    request = jnp.pad(tile_holder, ((0, 0), (0, 0), (0, 1)))
    request = jnp.where(place == columns, number, request)
    route = lax.all_to_all(request, ("depth", "view"), split_axis=0, concat_axis=0, tiled=True)
    route = route.reshape(plan.peers, columns + 1)
    stored = bricks[0, 0].reshape(columns, plan.zts, 8, plan.pairs, LANES).transpose(0, 1, 3, 2, 4)
    stored = stored.reshape(columns, plan.zts, 8, plan.regs, 8, LANES)
    early = march_early(plan, stored)
    messages = march_late(plan, stored, early, route)
    return finish(plan, exchange(plan, messages), route)


def solution(mesh):
    in_specs = (P("depth", "view", None, None, None), P("depth", "view", None))
    out_specs = P(None, "depth", "view")
    return jax.shard_map(body, mesh=mesh, in_specs=in_specs, out_specs=out_specs, check_vma=False)
```

```python
import functools

import jax
import jax.numpy as jnp
from jax import lax
from jax.experimental import pallas as pl
from jax.experimental.pallas import tpu as pltpu
from jax.sharding import PartitionSpec as P

STEPS = 48
DENSITY = 0.8
SHARPEN = 1.5
LANES = 128
PEERS = ("depth", "view")
VMEM_BYTES = 16 * 1024 * 1024


class Plan:
    def __init__(self, depths, views, columns, edge, area):
        self.depths, self.views, self.columns = depths, views, columns
        self.pairs = area // LANES
        self.band = self.pairs // depths
        self.rows = 4 * self.band + 6
        self.peers = depths * views
        self.zts = edge // 8
        self.regs = self.pairs // 8
        self.run = min(self.regs, self.band)
        self.tops = [a for a in range(self.regs) if a % self.band == 0]
        self.bottoms = [a for a in range(self.regs) if (a + 1) % self.run == 0][-len(self.tops) :]
        self.blocks = 3 if len(self.tops) == 1 else 4

    def peer(self, depth, view):
        return depth * self.views + view

    def run_of(self, band):
        pair = band * self.band
        return pair // self.regs, pair % self.regs


def roll(x, shift, axis=1):
    return pltpu.roll(x, shift % x.shape[axis], axis)


def lane_of(shape):
    return lax.broadcasted_iota(jnp.int32, shape, 1)


def march_tile(plan, load):
    scale = DENSITY / (2 * STEPS)
    regs = plan.regs
    lane = lane_of((8, LANES))
    row = lax.broadcasted_iota(jnp.int32, (8, LANES), 0)
    low = lane < 64
    inside = (lane % 64 != 0).astype(jnp.float32)
    top, bottom = row == 0, row == 7
    third = 1.0 / 3.0

    def three(zt, part):
        planes = [[load(zt, 4 * part + r, a) for a in range(regs)] for r in range(4)]
        first = [(5.0 * third) * p + third * q for p, q in zip(planes[0], planes[1])]
        second = [p + q for p, q in zip(planes[1], planes[2])]
        last = [third * p + (5.0 * third) * q for p, q in zip(planes[2], planes[3])]
        return [first, second, last]

    def step(index, behind, here, ahead, carry):
        turned = [roll(x, 64) for x in here]
        after = jnp.where(bottom, here[-1], roll(turned[0], -1, 0))
        steps_y = [y - x for x, y in zip(turned, turned[1:] + [after])]
        before = jnp.where(top, turned[0] - here[0], roll(steps_y[-1], 1, 0))
        steps_y = [before] + steps_y
        out = []
        for a in range(regs):
            total, trans, lit, red, blue = carry[a]
            x = here[a]
            grad_y = jnp.where(low, steps_y[a], steps_y[a + 1])
            diff = (x - roll(x, 1)) * inside
            grad_x = diff + roll(diff, -1)
            grad_z = ahead[a] - behind[a]
            norm = grad_x * grad_x + grad_y * grad_y + (grad_z * grad_z + 4.0)
            slope = jnp.abs(grad_z) * lax.rsqrt(norm)
            above = x - 2.0
            total = total + jnp.tanh(above)
            later = jnp.exp(total * -scale - scale * (index + 1))
            part = (trans - later) * (slope + 3.0 / 7.0)
            red = red + part * jnp.tanh(x * 0.375)
            blue = blue + part * jnp.tanh(above * 0.75)
            out.append((total, later, lit + part, red, blue))
        return out

    zero = jnp.zeros((8, LANES), jnp.float32)
    carry = [(zero, zero + 1.0, zero, zero, zero)] * regs
    samples = [x for zt in range(plan.zts) for part in range(2) for x in three(zt, part)]
    padded = samples[:1] + samples + samples[-1:]
    for index in range(STEPS):
        carry = step(index, *padded[index : index + 3], carry)
    value = [[], [], [], []]
    for _, trans, lit, red, blue in carry:
        value[0].append(0.35 * (lit + red))
        value[1].append(0.35 * (lit - red))
        value[2].append(0.35 * (lit + blue))
        value[3].append(1.0 - trans)
    return value


def store_tile(plan, value, tiles_ref, slot):
    regs = plan.regs
    lane = lane_of((8, LANES))
    low = lane < 64
    rows = [(c // 2, c % 2 * regs + a, value[c][a]) for c in range(4) for a in range(regs)]
    spot = 0
    for a in plan.tops:
        for c in (0, 2):
            edge = jnp.where(low, value[c][a], roll(value[c + 1][a], 64))
            rows.append((2 + spot // 8, spot % 8, edge))
            spot += 1
    for a in plan.bottoms:
        for c in (0, 2):
            edge = jnp.where(low, roll(value[c][a], 64), value[c + 1][a])
            rows.append((2 + spot // 8, spot % 8, edge))
            spot += 1
    for block, at, row in rows:
        tiles_ref[block, pl.ds(at, 8, 8), :] = row
    for number, column, base in ((0, 0, 0), (plan.columns - 1, 63, 4 * regs)):

        @pl.when(slot == number)
        def _():
            rim = jnp.zeros((8, LANES), jnp.float32)
            for c in range(4):
                for a in range(regs):
                    pixels = jnp.where(lane % 64 == column, value[c][a], 0.0)
                    rim += roll(pixels, base + 4 * a + c - column)
            tiles_ref[2 + spot // 8, pl.ds(spot % 8, 8, 8), :] = rim


def message_kernel(plan, view_ref, *refs):
    depths, views, columns = plan.depths, plan.views, plan.columns
    regs, run, band_pairs = plan.regs, plan.run, plan.band
    route_refs, (tiles_ref, out_ref, asked_ref) = refs[:-3], refs[-3:]
    view = view_ref[0]
    lane = lane_of((1, LANES))
    zero = jnp.zeros((1, LANES), jnp.float32)
    rim_at = 2 * len(plan.tops) + 2 * len(plan.bottoms)

    def rows_of(block, slot, sublane, at, count):
        return tiles_ref[block, pl.ds(slot * 64 + sublane * 8 + at, count), :]

    for i, route_ref in enumerate(route_refs):
        for r in range(2):
            found = jnp.int32(-1)
            for t in range(columns):
                found = jnp.where(route_ref[r, t] == view, t, found)
            asked_ref[view ^ (2 * i + r)] = found
    asked = [asked_ref[v] for v in range(views)]

    def rim(slot, sublane):
        return rows_of(2 + rim_at // 8, slot, sublane, rim_at % 8, 1)

    def above_of(band):
        sublane, a = plan.run_of(band)
        return (sublane, a - 1) if a > 0 else (sublane - 1, regs - 1)

    def below_of(band):
        sublane, a = plan.run_of(band)
        sublane, a = sublane + (a + band_pairs) // regs, (a + band_pairs) % regs
        return sublane, a

    own, corner = {}, {}
    for slot in (0, columns - 1):
        for band in range(depths):
            sublane, a = plan.run_of(band)
            total = zero
            for i in range(band_pairs // run):
                total = total + roll(rim(slot, sublane + i), 8 * regs * i - 4 * a)
            own[slot, band] = total
            total = zero
            if band > 0:
                sublane, a = above_of(band)
                moved = roll(rim(slot, sublane), 4 * (regs - 1 - a))
                keep = (lane % (4 * regs) >= 4 * (regs - 1)) & (lane >= 64)
                total = total + jnp.where(keep, moved, 0.0)
            if band < depths - 1:
                sublane, a = below_of(band)
                moved = roll(rim(slot, sublane), -4 * a)
                keep = (lane % (4 * regs) < 4) & (lane < 64)
                total = total + jnp.where(keep, moved, 0.0)
            corner[slot, band] = total

    for v in range(views):
        slot = jnp.maximum(asked[v], 0)
        sides = []
        if v + 1 < views:
            sides.append((0, jnp.where(asked[v + 1] == 0, 1.0, 0.0)))
        if v > 0:
            sides.append((columns - 1, jnp.where(asked[v - 1] == columns - 1, 1.0, 0.0)))
        for band in range(depths):
            at = plan.peer(band, v) * plan.rows
            first, a = plan.run_of(band)
            for c in range(4):
                for i in range(band_pairs // run):
                    start = at + c * band_pairs + i * run
                    out_ref[pl.ds(start, run), :] = rows_of(
                        c // 2, slot, first + i, c % 2 * regs + a, run
                    )
            at += 4 * band_pairs
            above = below = jnp.zeros((2, LANES), jnp.float32)
            if band > 0:
                sublane, a = above_of(band)
                place = 2 * len(plan.tops) + 2 * plan.bottoms.index(a)
                above = rows_of(2 + place // 8, slot, sublane, place % 8, 2)
            if band < depths - 1:
                sublane, a = below_of(band)
                place = 2 * plan.tops.index(a)
                below = rows_of(2 + place // 8, slot, sublane, place % 8, 2)
            out_ref[pl.ds(at, 2), :] = above
            out_ref[pl.ds(at + 2, 2), :] = below
            out_ref[pl.ds(at + 4, 1), :] = sum(own[s, band] * f for s, f in sides) + zero
            mark = jnp.where(lane == LANES - 1, asked[v].astype(jnp.float32), 0.0)
            out_ref[pl.ds(at + 5, 1), :] = sum(corner[s, band] * f for s, f in sides) + mark


def march_kernel(plan, x_ref, pair_ref, out_ref, held, sems):
    step = pl.program_id(0)

    def copies(slot):
        parity = slot % 2
        return [
            pltpu.make_async_copy(
                x_ref.at[slot, :, :, a], held.at[parity, :, a], sems.at[parity, a]
            )
            for a in range(plan.regs)
        ]

    @pl.when(step == 0)
    def _():
        for copy in copies(step):
            copy.start()

    @pl.when(step + 1 < plan.columns)
    def _():
        for copy in copies(step + 1):
            copy.start()

    for copy in copies(step):
        copy.wait()

    size = plan.zts * plan.regs * 64
    flat = held.reshape(2 * size, LANES)
    origin = (step % 2) * size

    def load(zt, r, a):
        return flat[pl.ds(origin + (zt * plan.regs + a) * 64 + r, 8, 8), :]

    store_tile(plan, march_tile(plan, load), out_ref, step)


SMEM = pl.BlockSpec(memory_space=pltpu.SMEM)
VMEM = pl.BlockSpec(memory_space=pltpu.VMEM)
PARAMS = pltpu.CompilerParams(vmem_limit_bytes=VMEM_BYTES)


def march(plan, stored, pair):
    samples = plan.columns * plan.pairs * LANES * STEPS
    return pl.pallas_call(
        functools.partial(march_kernel, plan),
        grid=(plan.columns,),
        in_specs=[pl.BlockSpec(memory_space=pltpu.HBM), pl.BlockSpec(memory_space=pl.ANY)],
        out_specs=pl.BlockSpec((plan.blocks, 64, LANES), lambda i: (0, i, 0)),
        out_shape=jax.ShapeDtypeStruct((plan.blocks, plan.columns * 64, LANES), jnp.float32),
        scratch_shapes=[
            pltpu.VMEM((2, plan.zts, plan.regs, 8, 8, LANES), jnp.float32),
            pltpu.SemaphoreType.DMA((2, plan.regs)),
        ],
        cost_estimate=pl.CostEstimate(
            flops=40 * samples, bytes_accessed=6 * samples, transcendentals=5 * samples
        ),
        compiler_params=pltpu.CompilerParams(vmem_limit_bytes=50*1024*1024),
        name="march",
    )(stored, pair)


def message(plan, view, routes, tiles):
    return pl.pallas_call(
        functools.partial(message_kernel, plan),
        in_specs=[SMEM] + [SMEM] * len(routes) + [VMEM],
        out_specs=VMEM,
        out_shape=jax.ShapeDtypeStruct((plan.peers * plan.rows, LANES), jnp.float32),
        scratch_shapes=[pltpu.SMEM((plan.views,), jnp.int32)],
        compiler_params=PARAMS,
        name="message",
    )(view, *routes, tiles)


def finish_kernel(plan, source, out_ref, image, marks):
    depths, views, band, columns = plan.depths, plan.views, plan.band, plan.columns
    regs = plan.regs
    lane = lane_of((1, LANES))
    low = lane < 64

    def over(front, alpha, back):
        return front if back is None else front + (1.0 - alpha) * back

    sides = None
    lane2 = lane_of((2, LANES))
    for d in reversed(range(depths)):
        front = None
        for h in range(views):
            n = plan.peer(d, h)
            piece = source[pl.ds(n * plan.rows + 4 * band + 4, 2), :]
            front = piece if front is None else front + piece
            mark = jnp.where(lane == LANES - 1, piece[1:2], 0.0)
            mark = jnp.sum(mark, axis=1, keepdims=True)
            marks[n] = jnp.broadcast_to(mark, (8, LANES))
        alpha = front
        for c in range(3):
            alpha = jnp.where(lane2 % 4 == c, roll(front, c - 3), alpha)
        sides = over(front, alpha, sides)

    bodies, outers = [], []
    low4 = lane_of((4, LANES)) < 64
    even4 = lax.broadcasted_iota(jnp.int32, (4, LANES), 0) % 2 == 0
    for t in range(columns):
        acc, rims = [None] * 4, None
        for d in reversed(range(depths)):
            front = [jnp.zeros((band, LANES), jnp.float32)] * 4
            rim = jnp.zeros((4, LANES), jnp.float32)
            for h in range(views):
                n = plan.peer(d, h)
                at = n * plan.rows
                chosen = marks[n] == t
                front = [
                    jnp.where(chosen[:band], source[pl.ds(at + c * band, band), :], x)
                    for c, x in enumerate(front)
                ]
                rim = jnp.where(chosen[:4], source[pl.ds(at + 4 * band, 4), :], rim)
            acc = [over(f, front[3], b) for f, b in zip(front, acc)]
            alpha = jnp.where(low4, roll(rim, 64), rim)
            alpha = jnp.where(even4, roll(alpha, -1, 0), alpha)
            rims = over(rim, alpha, rims)
        bodies.append(acc)
        outers.append([[rims[2 * side + i : 2 * side + i + 1] for i in range(2)] for side in range(2)])

    count = 2 * band
    wide = lane_of((band, LANES))
    low_band = wide < 64
    number = lax.broadcasted_iota(jnp.int32, (band, LANES), 0)
    number = 8 * regs * (number // regs) + 4 * (number % regs)
    final = columns // 2 + 1
    spread = jnp.broadcast_to(sides[0:1], (band, LANES))
    for c in range(4):
        for u in range(columns // 2):
            x, y = bodies[2 * u][c], bodies[2 * u + 1][c]
            image[c, u + 1, pl.ds(8, band, 2), :] = jnp.where(low_band, x, roll(y, 64))
            image[c, u + 1, pl.ds(9, band, 2), :] = jnp.where(low_band, roll(x, 64), y)
            for side, at in ((0, 7), (1, 8 + count)):
                x, y = outers[2 * u][side][c // 2], outers[2 * u + 1][side][c // 2]
                if c % 2 == 0:
                    y = roll(y, 64)
                else:
                    x = roll(x, 64)
                image[c, u + 1, pl.ds(at, 1), :] = jnp.where(low, x, y)
        for base, tile, spot in ((0, final, 0), (4 * regs, 0, LANES - 1)):
            for odd in range(2):
                here = wide == base + 64 * odd + number + c
                column = jnp.sum(jnp.where(here, spread, 0.0), axis=1, keepdims=True)
                image[c, tile, pl.ds(8 + odd, band, 2), :] = jnp.where(wide == spot, column, 0.0)
            for at, place in ((7, 64 + base + 4 * (regs - 1) + c), (8 + count, base + c)):
                pixel = jnp.where(lane == place, sides[1:2], 0.0)
                pixel = jnp.sum(pixel, axis=1, keepdims=True)
                image[c, tile, pl.ds(at, 1), :] = jnp.where(lane == spot, pixel, 0.0)

    full = lane_of((count, LANES))
    for c in range(4):
        middle = [image[c, k, pl.ds(8, count), :] for k in range(final + 1)]
        smooth = [
            0.25 * image[c, k, pl.ds(7, count), :]
            + 0.5 * middle[k]
            + 0.25 * image[c, k, pl.ds(9, count), :]
            for k in range(final + 1)
        ]
        later = [roll(x, 1) for x in smooth]
        sooner = [roll(x, -1) for x in smooth]
        for k in range(1, final):
            left = jnp.where(full == 0, later[k - 1], later[k])
            right = jnp.where(full == LANES - 1, sooner[k + 1], sooner[k])
            blurred = 0.25 * left + 0.5 * smooth[k] + 0.25 * right
            out_ref[c, :, pl.ds((k - 1) * LANES, LANES)] = middle[k] + SHARPEN * (
                middle[k] - blurred
            )


def finish(plan, arrived):
    count = 2 * plan.band
    return pl.pallas_call(
        functools.partial(finish_kernel, plan),
        in_specs=[VMEM],
        out_specs=VMEM,
        out_shape=jax.ShapeDtypeStruct((4, count, plan.columns * 64), jnp.float32),
        scratch_shapes=[
            pltpu.VMEM((4, plan.columns // 2 + 2, count + 16, LANES), jnp.float32),
            pltpu.VMEM((plan.peers, 8, LANES), jnp.float32),
        ],
        compiler_params=PARAMS,
        name="finish",
    )(arrived)


def exchange(plan, messages):
    cut = messages.reshape(plan.peers, plan.rows // 2, 2, LANES)
    moved = lax.all_to_all(cut, PEERS, split_axis=0, concat_axis=0, tiled=True)
    return moved.reshape(plan.peers * plan.rows, LANES)


def swapped(x, distance):
    pairs = [(i, i ^ distance) for i in range(lax.axis_size("view"))]
    return lax.ppermute(x, "view", pairs)


def body(bricks, tile_holder):
    depths, views = lax.axis_size("depth"), lax.axis_size("view")
    columns, edge, area = bricks.shape[2:]
    plan = Plan(depths, views, columns, edge, area)
    view = lax.axis_index("view").astype(jnp.int32).reshape(1)
    own = tile_holder.reshape(1, columns)
    pair = jnp.concatenate([own, swapped(own, 1)], axis=0)
    routes = [pair] + [swapped(pair, k) for k in range(2, views, 2)]
    stored = bricks[0, 0].reshape(columns, plan.zts, 8, plan.pairs, LANES).transpose(0, 1, 3, 2, 4)
    stored = stored.reshape(columns, plan.zts, 8, plan.regs, 8, LANES)
    messages = message(plan, view, routes, march(plan, stored, pair))
    return finish(plan, exchange(plan, messages))


def solution(mesh):
    in_specs = (P("depth", "view", None, None, None), P("depth", "view", None))
    out_specs = P(None, "depth", "view")
    return jax.shard_map(body, mesh=mesh, in_specs=in_specs, out_specs=out_specs, check_vma=False)
```

```python
import functools

import jax
import jax.numpy as jnp
from jax import lax
from jax.experimental import pallas as pl
from jax.experimental.pallas import tpu as pltpu
from jax.sharding import PartitionSpec as P

STEPS = 48
DENSITY = 0.8
SHARPEN = 1.5
LANES = 128
PEERS = ("depth", "view")
MARCH_BYTES = 50 * 1024 * 1024
FINISH_BYTES = 16 * 1024 * 1024
EARLY_PARTS = 2


class Plan:
    def __init__(self, depths, views, columns, edge, area):
        self.depths, self.views, self.columns = depths, views, columns
        self.pairs = area // LANES
        self.band = self.pairs // depths
        self.rows = 4 * self.band + 6
        self.peers = depths * views
        self.zts = edge // 8
        self.regs = self.pairs // 8
        self.run = min(self.regs, self.band)
        self.tops = [a for a in range(self.regs) if a % self.band == 0]
        self.bottoms = [a for a in range(self.regs) if (a + 1) % self.run == 0][-len(self.tops) :]
        self.blocks = 3 if len(self.tops) == 1 else 4

    def peer(self, depth, view):
        return depth * self.views + view

    def run_of(self, band):
        pair = band * self.band
        return pair // self.regs, pair % self.regs


def roll(x, shift, axis=1):
    return pltpu.roll(x, shift % x.shape[axis], axis)


def lane_of(shape):
    return lax.broadcasted_iota(jnp.int32, shape, 1)


def march_tile(plan, load, ready=lambda zt: None):
    scale = DENSITY / (2 * STEPS)
    regs = plan.regs
    lane = lane_of((8, LANES))
    row = lax.broadcasted_iota(jnp.int32, (8, LANES), 0)
    low = lane < 64
    inside = (lane % 64 != 0).astype(jnp.float32)
    top, bottom = row == 0, row == 7
    third = 1.0 / 3.0

    def three(zt, part):
        planes = [[load(zt, 4 * part + r, a) for a in range(regs)] for r in range(4)]
        first = [(5.0 * third) * p + third * q for p, q in zip(planes[0], planes[1])]
        second = [p + q for p, q in zip(planes[1], planes[2])]
        last = [third * p + (5.0 * third) * q for p, q in zip(planes[2], planes[3])]
        return [first, second, last]

    def step(index, behind, here, ahead, carry):
        turned = [roll(x, 64) for x in here]
        after = jnp.where(bottom, here[-1], roll(turned[0], -1, 0))
        steps_y = [y - x for x, y in zip(turned, turned[1:] + [after])]
        before = jnp.where(top, turned[0] - here[0], roll(steps_y[-1], 1, 0))
        steps_y = [before] + steps_y
        out = []
        for a in range(regs):
            total, trans, lit, red, blue = carry[a]
            x = here[a]
            grad_y = jnp.where(low, steps_y[a], steps_y[a + 1])
            diff = (x - roll(x, 1)) * inside
            grad_x = diff + roll(diff, -1)
            grad_z = ahead[a] - behind[a]
            norm = grad_x * grad_x + grad_y * grad_y + (grad_z * grad_z + 4.0)
            slope = jnp.abs(grad_z) * lax.rsqrt(norm)
            above = x - 2.0
            total = total + jnp.tanh(above)
            later = jnp.exp(total * -scale - scale * (index + 1))
            part = (trans - later) * (slope + 3.0 / 7.0)
            red = red + part * jnp.tanh(x * 0.375)
            blue = blue + part * jnp.tanh(above * 0.75)
            out.append((total, later, lit + part, red, blue))
        return out

    zero = jnp.zeros((8, LANES), jnp.float32)
    carry = [(zero, zero + 1.0, zero, zero, zero)] * regs
    samples, done = [], 0
    for zt in range(plan.zts):
        ready(zt)
        samples += three(zt, 0) + three(zt, 1)
        if zt == plan.zts - 1:
            samples.append(samples[-1])
        while done + 1 < len(samples):
            carry = step(done, samples[max(done - 1, 0)], *samples[done : done + 2], carry)
            done += 1
    value = [[], [], [], []]
    for _, trans, lit, red, blue in carry:
        value[0].append(0.35 * (lit + red))
        value[1].append(0.35 * (lit - red))
        value[2].append(0.35 * (lit + blue))
        value[3].append(1.0 - trans)
    return value


def store_tile(plan, value, tiles_ref, start):
    regs = plan.regs
    lane = lane_of((8, LANES))
    low = lane < 64
    rows = [(c // 2, c % 2 * regs + a, value[c][a]) for c in range(4) for a in range(regs)]
    spot = 0
    for a in plan.tops:
        for c in (0, 2):
            edge = jnp.where(low, value[c][a], roll(value[c + 1][a], 64))
            rows.append((2 + spot // 8, spot % 8, edge))
            spot += 1
    for a in plan.bottoms:
        for c in (0, 2):
            edge = jnp.where(low, roll(value[c][a], 64), value[c + 1][a])
            rows.append((2 + spot // 8, spot % 8, edge))
            spot += 1
    for block, at, row in rows:
        tiles_ref[block, pl.ds(start + at, 8, 8), :] = row


def store_rim(plan, value, tiles_ref, start, column, base):
    lane = lane_of((8, LANES))
    rim = jnp.zeros((8, LANES), jnp.float32)
    for c in range(4):
        for a in range(plan.regs):
            pixels = jnp.where(lane % 64 == column, value[c][a], 0.0)
            rim += roll(pixels, base + 4 * a + c - column)
    block, at = divmod(2 * len(plan.tops) + 2 * len(plan.bottoms), 8)
    tiles_ref[2 + block, pl.ds(start + at, 8, 8), :] = rim


def read_routes(plan, view, route_refs, asked_ref, order_ref):
    for i, route_ref in enumerate(route_refs):
        for r in range(2):
            found = jnp.int32(-1)
            for t in range(plan.columns):
                found = jnp.where(route_ref[r, t] == view, t, found)
            asked_ref[view ^ (2 * i + r)] = found
    asked = [asked_ref[v] for v in range(plan.views)]
    count = jnp.int32(0)
    for t in range(1, plan.columns):
        hit = functools.reduce(jnp.logical_or, [a == t for a in asked])
        order_ref[count + 1] = t
        count = count + jnp.where(hit, 1, 0)
    order_ref[0] = count


def assemble(plan, tiles_ref, asked_ref, out_ref):
    depths, views, columns = plan.depths, plan.views, plan.columns
    regs, run, band_pairs = plan.regs, plan.run, plan.band
    lane = lane_of((1, LANES))
    zero = jnp.zeros((1, LANES), jnp.float32)
    rim_at = 2 * len(plan.tops) + 2 * len(plan.bottoms)

    def rows_of(block, slot, sublane, at, count):
        return tiles_ref[block, pl.ds(slot * 64 + sublane * 8 + at, count), :]

    asked = [asked_ref[v] for v in range(views)]

    def rim(slot, sublane):
        return rows_of(2 + rim_at // 8, slot, sublane, rim_at % 8, 1)

    def above_of(band):
        sublane, a = plan.run_of(band)
        return (sublane, a - 1) if a > 0 else (sublane - 1, regs - 1)

    def below_of(band):
        sublane, a = plan.run_of(band)
        sublane, a = sublane + (a + band_pairs) // regs, (a + band_pairs) % regs
        return sublane, a

    own, corner = {}, {}
    for slot in (0, columns - 1):
        for band in range(depths):
            sublane, a = plan.run_of(band)
            total = zero
            for i in range(band_pairs // run):
                total = total + roll(rim(slot, sublane + i), 8 * regs * i - 4 * a)
            own[slot, band] = total
            total = zero
            if band > 0:
                sublane, a = above_of(band)
                moved = roll(rim(slot, sublane), 4 * (regs - 1 - a))
                keep = (lane % (4 * regs) >= 4 * (regs - 1)) & (lane >= 64)
                total = total + jnp.where(keep, moved, 0.0)
            if band < depths - 1:
                sublane, a = below_of(band)
                moved = roll(rim(slot, sublane), -4 * a)
                keep = (lane % (4 * regs) < 4) & (lane < 64)
                total = total + jnp.where(keep, moved, 0.0)
            corner[slot, band] = total

    for v in range(views):
        slot = jnp.maximum(asked[v], 0)
        sides = []
        if v + 1 < views:
            sides.append((0, asked[v + 1] == 0))
        if v > 0:
            sides.append((columns - 1, asked[v - 1] == columns - 1))
        for band in range(depths):
            at = plan.peer(band, v) * plan.rows
            first, a = plan.run_of(band)
            for c in range(4):
                for i in range(band_pairs // run):
                    start = at + c * band_pairs + i * run
                    out_ref[pl.ds(start, run), :] = rows_of(
                        c // 2, slot, first + i, c % 2 * regs + a, run
                    )
            at += 4 * band_pairs
            above = below = jnp.zeros((2, LANES), jnp.float32)
            if band > 0:
                sublane, a = above_of(band)
                place = 2 * len(plan.tops) + 2 * plan.bottoms.index(a)
                above = rows_of(2 + place // 8, slot, sublane, place % 8, 2)
            if band < depths - 1:
                sublane, a = below_of(band)
                place = 2 * plan.tops.index(a)
                below = rows_of(2 + place // 8, slot, sublane, place % 8, 2)
            out_ref[pl.ds(at, 2), :] = above
            out_ref[pl.ds(at + 2, 2), :] = below
            out_ref[pl.ds(at + 4, 1), :] = sum(jnp.where(f, own[s, band], 0.0) for s, f in sides) + zero
            mark = jnp.where(lane == LANES - 1, asked[v].astype(jnp.float32), 0.0)
            out_ref[pl.ds(at + 5, 1), :] = sum(jnp.where(f, corner[s, band], 0.0) for s, f in sides) + mark


def fetch(plan, x_ref, slot, held, sems, place, parts):
    size = plan.zts // parts
    return [
        [
            pltpu.make_async_copy(
                x_ref.at[slot, pl.ds(part * size, size), :, a],
                held.at[place, pl.ds(part * size, size), a],
                sems.at[place, part, a],
            )
            for a in range(plan.regs)
        ]
        for part in range(parts)
    ]


def loader(plan, held, place):
    size = plan.zts * plan.regs * 64
    flat = held.reshape(held.shape[0] * size, LANES)

    def load(zt, r, a):
        return flat[pl.ds(place * size + (zt * plan.regs + a) * 64 + r, 8, 8), :]

    return load


def early_kernel(plan, x_ref, pair_ref, tiles_ref, held, sems):
    parts = fetch(plan, x_ref, 0, held, sems, 0, EARLY_PARTS)
    for copies in parts:
        for copy in copies:
            copy.start()

    def ready(zt):
        if zt % (plan.zts // EARLY_PARTS) == 0:
            for copy in parts[zt // (plan.zts // EARLY_PARTS)]:
                copy.wait()

    value = march_tile(plan, loader(plan, held, 0), ready)
    store_tile(plan, value, tiles_ref, 0)
    store_rim(plan, value, tiles_ref, 0, 0, 0)


def late_kernel(plan, view_ref, *refs):
    route_refs, refs = refs[: plan.views // 2], refs[plan.views // 2 :]
    early_ref, x_ref, out_ref, tiles_ref, held, sems, early_sem, asked_ref, order_ref = refs
    step = pl.program_id(0)
    first = pltpu.make_async_copy(early_ref, tiles_ref.at[:, pl.ds(0, 64)], early_sem)

    def copies(number):
        slot = order_ref[number + 1]
        return fetch(plan, x_ref, slot, held, sems, number % 2, 1)[0]

    @pl.when(step == 0)
    def _():
        read_routes(plan, view_ref[0], route_refs, asked_ref, order_ref)

        @pl.when(order_ref[0] > 0)
        def _():
            for copy in copies(0):
                copy.start()

        first.start()

    @pl.when(step < order_ref[0])
    def _():
        @pl.when(step + 1 < order_ref[0])
        def _():
            for copy in copies(step + 1):
                copy.start()

        for copy in copies(step):
            copy.wait()
        value = march_tile(plan, loader(plan, held, step % 2))
        slot = order_ref[step + 1]
        start = pl.multiple_of(slot * 64, 64)
        store_tile(plan, value, tiles_ref, start)

        @pl.when(slot == plan.columns - 1)
        def _():
            store_rim(plan, value, tiles_ref, start, 63, 4 * plan.regs)

    @pl.when(step == plan.columns - 2)
    def _():
        first.wait()
        assemble(plan, tiles_ref, asked_ref, out_ref)


SMEM = pl.BlockSpec(memory_space=pltpu.SMEM)
VMEM = pl.BlockSpec(memory_space=pltpu.VMEM)
HBM = pl.BlockSpec(memory_space=pltpu.HBM)
ANY = pl.BlockSpec(memory_space=pl.ANY)


def granted(size):
    return pltpu.CompilerParams(vmem_limit_bytes=size)


def cost(plan, bricks):
    samples = bricks * plan.pairs * LANES * STEPS
    return pl.CostEstimate(
        flops=40 * samples, bytes_accessed=6 * samples, transcendentals=5 * samples
    )


def march_early(plan, stored, pair):
    return pl.pallas_call(
        functools.partial(early_kernel, plan),
        in_specs=[HBM, ANY],
        out_specs=VMEM,
        out_shape=jax.ShapeDtypeStruct((plan.blocks, 64, LANES), jnp.float32),
        scratch_shapes=[
            pltpu.VMEM((1, plan.zts, plan.regs, 8, 8, LANES), jnp.float32),
            pltpu.SemaphoreType.DMA((1, EARLY_PARTS, plan.regs)),
        ],
        cost_estimate=cost(plan, 1),
        compiler_params=granted(MARCH_BYTES),
        name="march_early",
    )(stored, pair)


def march_late(plan, view, routes, early, stored):
    shape = (plan.peers * plan.rows, LANES)
    return pl.pallas_call(
        functools.partial(late_kernel, plan),
        grid=(plan.columns - 1,),
        in_specs=[SMEM] + [SMEM] * len(routes) + [ANY, HBM],
        out_specs=pl.BlockSpec(shape, lambda i: (0, 0)),
        out_shape=jax.ShapeDtypeStruct(shape, jnp.float32),
        scratch_shapes=[
            pltpu.VMEM((plan.blocks, plan.columns * 64, LANES), jnp.float32),
            pltpu.VMEM((2, plan.zts, plan.regs, 8, 8, LANES), jnp.float32),
            pltpu.SemaphoreType.DMA((2, 1, plan.regs)),
            pltpu.SemaphoreType.DMA(()),
            pltpu.SMEM((plan.views,), jnp.int32),
            pltpu.SMEM((plan.columns + 1,), jnp.int32),
        ],
        cost_estimate=cost(plan, plan.columns - 1),
        compiler_params=granted(MARCH_BYTES),
        name="march_late",
    )(view, *routes, early, stored)


def finish_kernel(plan, source, out_ref, image, marks):
    depths, views, band, columns = plan.depths, plan.views, plan.band, plan.columns
    regs = plan.regs
    lane = lane_of((1, LANES))
    low = lane < 64

    def over(front, alpha, back):
        return front if back is None else front + (1.0 - alpha) * back

    sides = None
    lane2 = lane_of((2, LANES))
    for d in reversed(range(depths)):
        front = None
        for h in range(views):
            n = plan.peer(d, h)
            piece = source[pl.ds(n * plan.rows + 4 * band + 4, 2), :]
            front = piece if front is None else front + piece
            mark = jnp.where(lane == LANES - 1, piece[1:2], 0.0)
            mark = jnp.sum(mark, axis=1, keepdims=True)
            marks[n] = jnp.broadcast_to(mark, (8, LANES))
        alpha = front
        for c in range(3):
            alpha = jnp.where(lane2 % 4 == c, roll(front, c - 3), alpha)
        sides = over(front, alpha, sides)

    bodies, outers = [], []
    low4 = lane_of((4, LANES)) < 64
    even4 = lax.broadcasted_iota(jnp.int32, (4, LANES), 0) % 2 == 0
    for t in range(columns):
        acc, rims = [None] * 4, None
        for d in reversed(range(depths)):
            front = [jnp.zeros((band, LANES), jnp.float32)] * 4
            rim = jnp.zeros((4, LANES), jnp.float32)
            for h in range(views):
                n = plan.peer(d, h)
                at = n * plan.rows
                chosen = marks[n] == t
                front = [
                    jnp.where(chosen[:band], source[pl.ds(at + c * band, band), :], x)
                    for c, x in enumerate(front)
                ]
                rim = jnp.where(chosen[:4], source[pl.ds(at + 4 * band, 4), :], rim)
            acc = [over(f, front[3], b) for f, b in zip(front, acc)]
            alpha = jnp.where(low4, roll(rim, 64), rim)
            alpha = jnp.where(even4, roll(alpha, -1, 0), alpha)
            rims = over(rim, alpha, rims)
        bodies.append(acc)
        outers.append([[rims[2 * side + i : 2 * side + i + 1] for i in range(2)] for side in range(2)])

    count = 2 * band
    wide = lane_of((band, LANES))
    low_band = wide < 64
    number = lax.broadcasted_iota(jnp.int32, (band, LANES), 0)
    number = 8 * regs * (number // regs) + 4 * (number % regs)
    final = columns // 2 + 1
    spread = jnp.broadcast_to(sides[0:1], (band, LANES))
    for c in range(4):
        for u in range(columns // 2):
            x, y = bodies[2 * u][c], bodies[2 * u + 1][c]
            image[c, u + 1, pl.ds(8, band, 2), :] = jnp.where(low_band, x, roll(y, 64))
            image[c, u + 1, pl.ds(9, band, 2), :] = jnp.where(low_band, roll(x, 64), y)
            for side, at in ((0, 7), (1, 8 + count)):
                x, y = outers[2 * u][side][c // 2], outers[2 * u + 1][side][c // 2]
                if c % 2 == 0:
                    y = roll(y, 64)
                else:
                    x = roll(x, 64)
                image[c, u + 1, pl.ds(at, 1), :] = jnp.where(low, x, y)
        for base, tile, spot in ((0, final, 0), (4 * regs, 0, LANES - 1)):
            for odd in range(2):
                here = wide == base + 64 * odd + number + c
                column = jnp.sum(jnp.where(here, spread, 0.0), axis=1, keepdims=True)
                image[c, tile, pl.ds(8 + odd, band, 2), :] = jnp.where(wide == spot, column, 0.0)
            for at, place in ((7, 64 + base + 4 * (regs - 1) + c), (8 + count, base + c)):
                pixel = jnp.where(lane == place, sides[1:2], 0.0)
                pixel = jnp.sum(pixel, axis=1, keepdims=True)
                image[c, tile, pl.ds(at, 1), :] = jnp.where(lane == spot, pixel, 0.0)

    full = lane_of((count, LANES))
    for c in range(4):
        middle = [image[c, k, pl.ds(8, count), :] for k in range(final + 1)]
        smooth = [
            0.25 * image[c, k, pl.ds(7, count), :]
            + 0.5 * middle[k]
            + 0.25 * image[c, k, pl.ds(9, count), :]
            for k in range(final + 1)
        ]
        later = [roll(x, 1) for x in smooth]
        sooner = [roll(x, -1) for x in smooth]
        for k in range(1, final):
            left = jnp.where(full == 0, later[k - 1], later[k])
            right = jnp.where(full == LANES - 1, sooner[k + 1], sooner[k])
            blurred = 0.25 * left + 0.5 * smooth[k] + 0.25 * right
            out_ref[c, :, pl.ds((k - 1) * LANES, LANES)] = middle[k] + SHARPEN * (
                middle[k] - blurred
            )


def finish(plan, arrived):
    count = 2 * plan.band
    return pl.pallas_call(
        functools.partial(finish_kernel, plan),
        in_specs=[VMEM],
        out_specs=VMEM,
        out_shape=jax.ShapeDtypeStruct((4, count, plan.columns * 64), jnp.float32),
        scratch_shapes=[
            pltpu.VMEM((4, plan.columns // 2 + 2, count + 16, LANES), jnp.float32),
            pltpu.VMEM((plan.peers, 8, LANES), jnp.float32),
        ],
        compiler_params=granted(FINISH_BYTES),
        name="finish",
    )(arrived)


def exchange(plan, messages):
    cut = messages.reshape(plan.peers, plan.rows // 2, 2, LANES)
    moved = lax.all_to_all(cut, PEERS, split_axis=0, concat_axis=0, tiled=True)
    return moved.reshape(plan.peers * plan.rows, LANES)


def swapped(x, distance):
    pairs = [(i, i ^ distance) for i in range(lax.axis_size("view"))]
    return lax.ppermute(x, "view", pairs)


def body(bricks, tile_holder):
    depths, views = lax.axis_size("depth"), lax.axis_size("view")
    columns, edge, area = bricks.shape[2:]
    plan = Plan(depths, views, columns, edge, area)
    view = lax.axis_index("view").astype(jnp.int32).reshape(1)
    own = tile_holder.reshape(1, columns)
    pair = jnp.concatenate([own, swapped(own, 1)], axis=0)
    routes = [pair] + [swapped(pair, k) for k in range(2, views, 2)]
    stored = bricks[0, 0].reshape(columns, plan.zts, 8, plan.pairs, LANES).transpose(0, 1, 3, 2, 4)
    stored = stored.reshape(columns, plan.zts, 8, plan.regs, 8, LANES)
    early = march_early(plan, stored, pair)
    messages = march_late(plan, view, routes, early, stored)
    return finish(plan, exchange(plan, messages))


def solution(mesh):
    in_specs = (P("depth", "view", None, None, None), P("depth", "view", None))
    out_specs = P(None, "depth", "view")
    return jax.shard_map(body, mesh=mesh, in_specs=in_specs, out_specs=out_specs, check_vma=False)
```

```python
import functools

import jax
import jax.numpy as jnp
from jax import lax
from jax.experimental import pallas as pl
from jax.experimental.pallas import tpu as pltpu
from jax.sharding import PartitionSpec as P

STEPS = 48
DENSITY = 0.8
SHARPEN = 1.5
LANES = 128
PEERS = ("depth", "view")
MARCH_BYTES = 50 * 1024 * 1024
FINISH_BYTES = 16 * 1024 * 1024
EARLY_PARTS = 2


class Plan:
    def __init__(self, depths, views, columns, edge, area):
        self.depths, self.views, self.columns = depths, views, columns
        self.pairs = area // LANES
        self.band = self.pairs // depths
        self.rows = 4 * self.band + 6
        self.peers = depths * views
        self.zts = edge // 8
        self.regs = self.pairs // 8
        self.run = min(self.regs, self.band)
        self.tops = [a for a in range(self.regs) if a % self.band == 0]
        self.bottoms = [a for a in range(self.regs) if (a + 1) % self.run == 0][-len(self.tops) :]
        self.blocks = 3 if len(self.tops) == 1 else 4

    def peer(self, depth, view):
        return depth * self.views + view

    def run_of(self, band):
        pair = band * self.band
        return pair // self.regs, pair % self.regs


def roll(x, shift, axis=1):
    return pltpu.roll(x, shift % x.shape[axis], axis)


def lane_of(shape):
    return lax.broadcasted_iota(jnp.int32, shape, 1)


def march_tile(plan, load, ready=lambda zt: None):
    scale = DENSITY / (2 * STEPS)
    regs = plan.regs
    lane = lane_of((8, LANES))
    row = lax.broadcasted_iota(jnp.int32, (8, LANES), 0)
    low = lane < 64
    inside = (lane % 64 != 0).astype(jnp.float32)
    top, bottom = row == 0, row == 7
    third = 1.0 / 3.0

    def three(zt, part):
        planes = [[load(zt, 4 * part + r, a) for a in range(regs)] for r in range(4)]
        first = [(5.0 * third) * p + third * q for p, q in zip(planes[0], planes[1])]
        second = [p + q for p, q in zip(planes[1], planes[2])]
        last = [third * p + (5.0 * third) * q for p, q in zip(planes[2], planes[3])]
        return [first, second, last]

    def step(index, behind, here, ahead, carry):
        turned = [roll(x, 64) for x in here]
        after = jnp.where(bottom, here[-1], roll(turned[0], -1, 0))
        steps_y = [y - x for x, y in zip(turned, turned[1:] + [after])]
        before = jnp.where(top, turned[0] - here[0], roll(steps_y[-1], 1, 0))
        steps_y = [before] + steps_y
        out = []
        for a in range(regs):
            total, trans, lit, red, blue = carry[a]
            x = here[a]
            grad_y = jnp.where(low, steps_y[a], steps_y[a + 1])
            diff = (x - roll(x, 1)) * inside
            grad_x = diff + roll(diff, -1)
            grad_z = ahead[a] - behind[a]
            norm = grad_x * grad_x + grad_y * grad_y + (grad_z * grad_z + 4.0)
            slope = jnp.abs(grad_z) * lax.rsqrt(norm)
            above = x - 2.0
            total = total + jnp.tanh(above)
            later = jnp.exp(total * -scale - scale * (index + 1))
            part = (trans - later) * (slope + 3.0 / 7.0)
            red = red + part * jnp.tanh(x * 0.375)
            blue = blue + part * jnp.tanh(above * 0.75)
            out.append((total, later, lit + part, red, blue))
        return out

    zero = jnp.zeros((8, LANES), jnp.float32)
    carry = [(zero, zero + 1.0, zero, zero, zero)] * regs
    samples, done = [], 0
    for zt in range(plan.zts):
        ready(zt)
        samples += three(zt, 0) + three(zt, 1)
        if zt == plan.zts - 1:
            samples.append(samples[-1])
        while done + 1 < len(samples):
            carry = step(done, samples[max(done - 1, 0)], *samples[done : done + 2], carry)
            done += 1
    value = [[], [], [], []]
    for _, trans, lit, red, blue in carry:
        value[0].append(0.35 * (lit + red))
        value[1].append(0.35 * (lit - red))
        value[2].append(0.35 * (lit + blue))
        value[3].append(1.0 - trans)
    return value


def store_tile(plan, value, tiles_ref, start):
    regs = plan.regs
    lane = lane_of((8, LANES))
    low = lane < 64
    rows = [(c // 2, c % 2 * regs + a, value[c][a]) for c in range(4) for a in range(regs)]
    spot = 0
    for a in plan.tops:
        for c in (0, 2):
            edge = jnp.where(low, value[c][a], roll(value[c + 1][a], 64))
            rows.append((2 + spot // 8, spot % 8, edge))
            spot += 1
    for a in plan.bottoms:
        for c in (0, 2):
            edge = jnp.where(low, roll(value[c][a], 64), value[c + 1][a])
            rows.append((2 + spot // 8, spot % 8, edge))
            spot += 1
    for block, at, row in rows:
        tiles_ref[block, pl.ds(start + at, 8, 8), :] = row


def store_rim(plan, value, tiles_ref, start, column, base):
    lane = lane_of((8, LANES))
    rim = jnp.zeros((8, LANES), jnp.float32)
    for c in range(4):
        for a in range(plan.regs):
            pixels = jnp.where(lane % 64 == column, value[c][a], 0.0)
            rim += roll(pixels, base + 4 * a + c - column)
    block, at = divmod(2 * len(plan.tops) + 2 * len(plan.bottoms), 8)
    tiles_ref[2 + block, pl.ds(start + at, 8, 8), :] = rim


def read_routes(plan, view, route_refs, asked_ref, order_ref):
    for i, route_ref in enumerate(route_refs):
        for r in range(2):
            found = jnp.int32(-1)
            for t in range(plan.columns):
                found = jnp.where(route_ref[r, t] == view, t, found)
            asked_ref[view ^ (2 * i + r)] = found
    asked = [asked_ref[v] for v in range(plan.views)]
    count = jnp.int32(0)
    for t in range(1, plan.columns):
        hit = functools.reduce(jnp.logical_or, [a == t for a in asked])
        order_ref[count + 1] = t
        count = count + jnp.where(hit, 1, 0)
    order_ref[0] = count


def assemble(plan, tiles_ref, asked_ref, out_ref):
    depths, views, columns = plan.depths, plan.views, plan.columns
    regs, run, band_pairs = plan.regs, plan.run, plan.band
    lane = lane_of((1, LANES))
    zero = jnp.zeros((1, LANES), jnp.float32)
    rim_at = 2 * len(plan.tops) + 2 * len(plan.bottoms)

    def rows_of(block, slot, sublane, at, count):
        return tiles_ref[block, pl.ds(slot * 64 + sublane * 8 + at, count), :]

    asked = [asked_ref[v] for v in range(views)]

    def rim(slot, sublane):
        return rows_of(2 + rim_at // 8, slot, sublane, rim_at % 8, 1)

    def above_of(band):
        sublane, a = plan.run_of(band)
        return (sublane, a - 1) if a > 0 else (sublane - 1, regs - 1)

    def below_of(band):
        sublane, a = plan.run_of(band)
        sublane, a = sublane + (a + band_pairs) // regs, (a + band_pairs) % regs
        return sublane, a

    own, corner = {}, {}
    for slot in (0, columns - 1):
        for band in range(depths):
            sublane, a = plan.run_of(band)
            total = zero
            for i in range(band_pairs // run):
                total = total + roll(rim(slot, sublane + i), 8 * regs * i - 4 * a)
            own[slot, band] = total
            total = zero
            if band > 0:
                sublane, a = above_of(band)
                moved = roll(rim(slot, sublane), 4 * (regs - 1 - a))
                keep = (lane % (4 * regs) >= 4 * (regs - 1)) & (lane >= 64)
                total = total + jnp.where(keep, moved, 0.0)
            if band < depths - 1:
                sublane, a = below_of(band)
                moved = roll(rim(slot, sublane), -4 * a)
                keep = (lane % (4 * regs) < 4) & (lane < 64)
                total = total + jnp.where(keep, moved, 0.0)
            corner[slot, band] = total

    for v in range(views):
        slot = jnp.maximum(asked[v], 0)
        sides = []
        if v + 1 < views:
            sides.append((0, asked[v + 1] == 0))
        if v > 0:
            sides.append((columns - 1, asked[v - 1] == columns - 1))
        for band in range(depths):
            at = plan.peer(band, v) * plan.rows
            first, a = plan.run_of(band)
            for c in range(4):
                for i in range(band_pairs // run):
                    start = at + c * band_pairs + i * run
                    out_ref[pl.ds(start, run), :] = rows_of(
                        c // 2, slot, first + i, c % 2 * regs + a, run
                    )
            at += 4 * band_pairs
            above = below = jnp.zeros((2, LANES), jnp.float32)
            if band > 0:
                sublane, a = above_of(band)
                place = 2 * len(plan.tops) + 2 * plan.bottoms.index(a)
                above = rows_of(2 + place // 8, slot, sublane, place % 8, 2)
            if band < depths - 1:
                sublane, a = below_of(band)
                place = 2 * plan.tops.index(a)
                below = rows_of(2 + place // 8, slot, sublane, place % 8, 2)
            out_ref[pl.ds(at, 2), :] = above
            out_ref[pl.ds(at + 2, 2), :] = below
            out_ref[pl.ds(at + 4, 1), :] = sum(jnp.where(f, own[s, band], 0.0) for s, f in sides) + zero
            mark = jnp.where(lane == LANES - 1, asked[v].astype(jnp.float32), 0.0)
            out_ref[pl.ds(at + 5, 1), :] = sum(jnp.where(f, corner[s, band], 0.0) for s, f in sides) + mark


def fetch(plan, x_ref, slot, held, sems, place, parts):
    size = plan.zts // parts
    return [
        [
            pltpu.make_async_copy(
                x_ref.at[slot, pl.ds(part * size, size), :, a],
                held.at[place, pl.ds(part * size, size), a],
                sems.at[place, part, a],
            )
            for a in range(plan.regs)
        ]
        for part in range(parts)
    ]


def loader(plan, held, place):
    size = plan.zts * plan.regs * 64
    flat = held.reshape(held.shape[0] * size, LANES)

    def load(zt, r, a):
        return flat[pl.ds(place * size + (zt * plan.regs + a) * 64 + r, 8, 8), :]

    return load


def early_kernel(plan, x_ref, pair_ref, tiles_ref, held, sems):
    parts = fetch(plan, x_ref, 0, held, sems, 0, EARLY_PARTS)
    for copies in parts:
        for copy in copies:
            copy.start()

    def ready(zt):
        if zt % (plan.zts // EARLY_PARTS) == 0:
            for copy in parts[zt // (plan.zts // EARLY_PARTS)]:
                copy.wait()

    value = march_tile(plan, loader(plan, held, 0), ready)
    store_tile(plan, value, tiles_ref, 0)
    store_rim(plan, value, tiles_ref, 0, 0, 0)


def late_kernel(plan, view_ref, *refs):
    route_refs, refs = refs[: plan.views // 2], refs[plan.views // 2 :]
    early_ref, x_ref, out_ref, tiles_ref, held, sems, early_sem, asked_ref, order_ref = refs
    first = pltpu.make_async_copy(early_ref, tiles_ref.at[:, pl.ds(0, 64)], early_sem)
    first.start()
    read_routes(plan, view_ref[0], route_refs, asked_ref, order_ref)
    count = order_ref[0]

    def copies(number):
        slot = order_ref[number + 1]
        return fetch(plan, x_ref, slot, held, sems, number % 2, 1)[0]

    @pl.when(count > 0)
    def _():
        for copy in copies(0):
            copy.start()

    def step(number, carry):
        @pl.when(number + 1 < count)
        def _():
            for copy in copies(number + 1):
                copy.start()

        for copy in copies(number):
            copy.wait()
        value = march_tile(plan, loader(plan, held, number % 2))
        slot = order_ref[number + 1]
        start = pl.multiple_of(slot * 64, 64)
        store_tile(plan, value, tiles_ref, start)

        @pl.when(slot == plan.columns - 1)
        def _():
            store_rim(plan, value, tiles_ref, start, 63, 4 * plan.regs)

        return carry

    lax.fori_loop(0, count, step, 0)
    first.wait()
    assemble(plan, tiles_ref, asked_ref, out_ref)


SMEM = pl.BlockSpec(memory_space=pltpu.SMEM)
VMEM = pl.BlockSpec(memory_space=pltpu.VMEM)
HBM = pl.BlockSpec(memory_space=pltpu.HBM)
ANY = pl.BlockSpec(memory_space=pl.ANY)


def granted(size):
    return pltpu.CompilerParams(vmem_limit_bytes=size)


def cost(plan, bricks):
    samples = bricks * plan.pairs * LANES * STEPS
    return pl.CostEstimate(
        flops=40 * samples, bytes_accessed=6 * samples, transcendentals=5 * samples
    )


def march_early(plan, stored, pair):
    return pl.pallas_call(
        functools.partial(early_kernel, plan),
        in_specs=[HBM, ANY],
        out_specs=VMEM,
        out_shape=jax.ShapeDtypeStruct((plan.blocks, 64, LANES), jnp.float32),
        scratch_shapes=[
            pltpu.VMEM((1, plan.zts, plan.regs, 8, 8, LANES), jnp.float32),
            pltpu.SemaphoreType.DMA((1, EARLY_PARTS, plan.regs)),
        ],
        cost_estimate=cost(plan, 1),
        compiler_params=granted(MARCH_BYTES),
        name="march_early",
    )(stored, pair)


def march_late(plan, view, routes, early, stored):
    shape = (plan.peers * plan.rows, LANES)
    return pl.pallas_call(
        functools.partial(late_kernel, plan),
        in_specs=[SMEM] + [SMEM] * len(routes) + [ANY, HBM],
        out_specs=VMEM,
        out_shape=jax.ShapeDtypeStruct(shape, jnp.float32),
        scratch_shapes=[
            pltpu.VMEM((plan.blocks, plan.columns * 64, LANES), jnp.float32),
            pltpu.VMEM((2, plan.zts, plan.regs, 8, 8, LANES), jnp.float32),
            pltpu.SemaphoreType.DMA((2, 1, plan.regs)),
            pltpu.SemaphoreType.DMA(()),
            pltpu.SMEM((plan.views,), jnp.int32),
            pltpu.SMEM((plan.columns + 1,), jnp.int32),
        ],
        cost_estimate=cost(plan, plan.columns - 1),
        compiler_params=granted(MARCH_BYTES),
        name="march_late",
    )(view, *routes, early, stored)


def finish_kernel(plan, source, out_ref, image, marks):
    depths, views, band, columns = plan.depths, plan.views, plan.band, plan.columns
    regs = plan.regs
    lane = lane_of((1, LANES))
    low = lane < 64

    def over(front, alpha, back):
        return front if back is None else front + (1.0 - alpha) * back

    sides = None
    lane2 = lane_of((2, LANES))
    for d in reversed(range(depths)):
        front = None
        for h in range(views):
            n = plan.peer(d, h)
            piece = source[pl.ds(n * plan.rows + 4 * band + 4, 2), :]
            front = piece if front is None else front + piece
            mark = jnp.where(lane == LANES - 1, piece[1:2], 0.0)
            mark = jnp.sum(mark, axis=1, keepdims=True)
            marks[n] = jnp.broadcast_to(mark, (8, LANES))
        alpha = front
        for c in range(3):
            alpha = jnp.where(lane2 % 4 == c, roll(front, c - 3), alpha)
        sides = over(front, alpha, sides)

    bodies, outers = [], []
    low8 = lane_of((8, LANES)) < 64
    even8 = lax.broadcasted_iota(jnp.int32, (8, LANES), 0) % 2 == 0
    for t in range(columns):
        acc, rims = [None] * 4, None
        for d in reversed(range(depths)):
            front = [jnp.zeros((band, LANES), jnp.float32)] * 4
            rim = jnp.zeros((8, LANES), jnp.float32)
            for h in range(views):
                n = plan.peer(d, h)
                at = n * plan.rows
                chosen = marks[n] == t
                front = [
                    jnp.where(chosen[:band], source[pl.ds(at + c * band, band), :], x)
                    for c, x in enumerate(front)
                ]
                rim = jnp.where(chosen, source[pl.ds(at + 4 * band - 2, 8), :], rim)
            acc = [over(f, front[3], b) for f, b in zip(front, acc)]
            alpha = jnp.where(low8, roll(rim, 64), rim)
            alpha = jnp.where(even8, roll(alpha, -1, 0), alpha)
            rims = over(rim, alpha, rims)
        bodies.append(acc)
        outers.append([[rims[2 * side + i + 2 : 2 * side + i + 3] for i in range(2)] for side in range(2)])

    count = 2 * band
    wide = lane_of((band, LANES))
    low_band = wide < 64
    number = lax.broadcasted_iota(jnp.int32, (band, LANES), 0)
    number = 8 * regs * (number // regs) + 4 * (number % regs)
    final = columns // 2 + 1
    spread = jnp.broadcast_to(sides[0:1], (band, LANES))
    for c in range(4):
        for u in range(columns // 2):
            x, y = bodies[2 * u][c], bodies[2 * u + 1][c]
            image[c, u + 1, pl.ds(8, band, 2), :] = jnp.where(low_band, x, roll(y, 64))
            image[c, u + 1, pl.ds(9, band, 2), :] = jnp.where(low_band, roll(x, 64), y)
            for side, at in ((0, 7), (1, 8 + count)):
                x, y = outers[2 * u][side][c // 2], outers[2 * u + 1][side][c // 2]
                if c % 2 == 0:
                    y = roll(y, 64)
                else:
                    x = roll(x, 64)
                image[c, u + 1, pl.ds(at, 1), :] = jnp.where(low, x, y)
        for base, tile, spot in ((0, final, 0), (4 * regs, 0, LANES - 1)):
            for odd in range(2):
                here = wide == base + 64 * odd + number + c
                column = jnp.sum(jnp.where(here, spread, 0.0), axis=1, keepdims=True)
                image[c, tile, pl.ds(8 + odd, band, 2), :] = jnp.where(wide == spot, column, 0.0)
            for at, place in ((7, 64 + base + 4 * (regs - 1) + c), (8 + count, base + c)):
                pixel = jnp.where(lane == place, sides[1:2], 0.0)
                pixel = jnp.sum(pixel, axis=1, keepdims=True)
                image[c, tile, pl.ds(at, 1), :] = jnp.where(lane == spot, pixel, 0.0)

    full = lane_of((count, LANES))
    for c in range(4):
        middle = [image[c, k, pl.ds(8, count), :] for k in range(final + 1)]
        smooth = [
            0.25 * image[c, k, pl.ds(7, count), :]
            + 0.5 * middle[k]
            + 0.25 * image[c, k, pl.ds(9, count), :]
            for k in range(final + 1)
        ]
        later = [roll(x, 1) for x in smooth]
        sooner = [roll(x, -1) for x in smooth]
        for k in range(1, final):
            left = jnp.where(full == 0, later[k - 1], later[k])
            right = jnp.where(full == LANES - 1, sooner[k + 1], sooner[k])
            blurred = 0.25 * left + 0.5 * smooth[k] + 0.25 * right
            out_ref[c, :, pl.ds((k - 1) * LANES, LANES)] = middle[k] + SHARPEN * (
                middle[k] - blurred
            )


def finish(plan, arrived):
    count = 2 * plan.band
    return pl.pallas_call(
        functools.partial(finish_kernel, plan),
        in_specs=[VMEM],
        out_specs=VMEM,
        out_shape=jax.ShapeDtypeStruct((4, count, plan.columns * 64), jnp.float32),
        scratch_shapes=[
            pltpu.VMEM((4, plan.columns // 2 + 2, count + 16, LANES), jnp.float32),
            pltpu.VMEM((plan.peers, 8, LANES), jnp.float32),
        ],
        compiler_params=granted(FINISH_BYTES),
        name="finish",
    )(arrived)


def exchange(plan, messages):
    cut = messages.reshape(plan.peers, plan.rows // 2, 2, LANES)
    moved = lax.all_to_all(cut, PEERS, split_axis=0, concat_axis=0, tiled=True)
    return moved.reshape(plan.peers * plan.rows, LANES)


def swapped(x, distance):
    pairs = [(i, i ^ distance) for i in range(lax.axis_size("view"))]
    return lax.ppermute(x, "view", pairs)


def body(bricks, tile_holder):
    depths, views = lax.axis_size("depth"), lax.axis_size("view")
    columns, edge, area = bricks.shape[2:]
    plan = Plan(depths, views, columns, edge, area)
    view = lax.axis_index("view").astype(jnp.int32).reshape(1)
    own = tile_holder.reshape(1, columns)
    pair = jnp.concatenate([own, swapped(own, 1)], axis=0)
    routes = [pair] + [swapped(pair, k) for k in range(2, views, 2)]
    stored = bricks[0, 0].reshape(columns, plan.zts, 8, plan.pairs, LANES).transpose(0, 1, 3, 2, 4)
    stored = stored.reshape(columns, plan.zts, 8, plan.regs, 8, LANES)
    early = march_early(plan, stored, pair)
    messages = march_late(plan, view, routes, early, stored)
    return finish(plan, exchange(plan, messages))


def solution(mesh):
    in_specs = (P("depth", "view", None, None, None), P("depth", "view", None))
    out_specs = P(None, "depth", "view")
    return jax.shard_map(body, mesh=mesh, in_specs=in_specs, out_specs=out_specs, check_vma=False)
```

```python
import functools

import jax
import jax.numpy as jnp
from jax import lax
from jax.experimental import pallas as pl
from jax.experimental.pallas import tpu as pltpu
from jax.sharding import PartitionSpec as P

STEPS = 48
DENSITY = 0.8
SHARPEN = 1.5
LANES = 128
PEERS = ("depth", "view")
MARCH_BYTES = 50 * 1024 * 1024
FINISH_BYTES = 16 * 1024 * 1024
EARLY_PARTS = 2


class Plan:
    def __init__(self, depths, views, columns, edge, area):
        self.depths, self.views, self.columns = depths, views, columns
        self.pairs = area // LANES
        self.band = self.pairs // depths
        self.rows = 4 * self.band + 6
        self.peers = depths * views
        self.zts = edge // 8
        self.regs = self.pairs // 8
        self.run = min(self.regs, self.band)
        self.tops = [a for a in range(self.regs) if a % self.band == 0]
        self.bottoms = [a for a in range(self.regs) if (a + 1) % self.run == 0][-len(self.tops) :]
        self.blocks = 3 if len(self.tops) == 1 else 4

    def peer(self, depth, view):
        return depth * self.views + view

    def run_of(self, band):
        pair = band * self.band
        return pair // self.regs, pair % self.regs


def roll(x, shift, axis=1):
    return pltpu.roll(x, shift % x.shape[axis], axis)


def lane_of(shape):
    return lax.broadcasted_iota(jnp.int32, shape, 1)


def march_tile(plan, load, ready=lambda zt: None):
    scale = DENSITY / (2 * STEPS)
    regs = plan.regs
    lane = lane_of((8, LANES))
    row = lax.broadcasted_iota(jnp.int32, (8, LANES), 0)
    low = lane < 64
    inside = (lane % 64 != 0).astype(jnp.float32)
    top, bottom = row == 0, row == 7
    third = 1.0 / 3.0

    def three(zt, part):
        planes = [[load(zt, 4 * part + r, a) for a in range(regs)] for r in range(4)]
        first = [(5.0 * third) * p + third * q for p, q in zip(planes[0], planes[1])]
        second = [p + q for p, q in zip(planes[1], planes[2])]
        last = [third * p + (5.0 * third) * q for p, q in zip(planes[2], planes[3])]
        return [first, second, last]

    def step(index, behind, here, ahead, carry):
        turned = [roll(x, 64) for x in here]
        after = jnp.where(bottom, here[-1], roll(turned[0], -1, 0))
        steps_y = [y - x for x, y in zip(turned, turned[1:] + [after])]
        before = jnp.where(top, turned[0] - here[0], roll(steps_y[-1], 1, 0))
        steps_y = [before] + steps_y
        out = []
        for a in range(regs):
            total, trans, lit, red, blue = carry[a]
            x = here[a]
            grad_y = jnp.where(low, steps_y[a], steps_y[a + 1])
            diff = (x - roll(x, 1)) * inside
            grad_x = diff + roll(diff, -1)
            grad_z = ahead[a] - behind[a]
            norm = grad_x * grad_x + grad_y * grad_y + (grad_z * grad_z + 4.0)
            slope = jnp.abs(grad_z) * lax.rsqrt(norm)
            above = x - 2.0
            total = total + jnp.tanh(above)
            later = jnp.exp(total * -scale - scale * (index + 1))
            part = (trans - later) * (slope + 3.0 / 7.0)
            red = red + part * jnp.tanh(x * 0.375)
            blue = blue + part * jnp.tanh(above * 0.75)
            out.append((total, later, lit + part, red, blue))
        return out

    zero = jnp.zeros((8, LANES), jnp.float32)
    carry = [(zero, zero + 1.0, zero, zero, zero)] * regs
    samples, done = [], 0
    for zt in range(plan.zts):
        ready(zt)
        samples += three(zt, 0) + three(zt, 1)
        if zt == plan.zts - 1:
            samples.append(samples[-1])
        while done + 1 < len(samples):
            carry = step(done, samples[max(done - 1, 0)], *samples[done : done + 2], carry)
            done += 1
    value = [[], [], [], []]
    for _, trans, lit, red, blue in carry:
        value[0].append(0.35 * (lit + red))
        value[1].append(0.35 * (lit - red))
        value[2].append(0.35 * (lit + blue))
        value[3].append(1.0 - trans)
    return value


def store_tile(plan, value, tiles_ref, start):
    regs = plan.regs
    lane = lane_of((8, LANES))
    low = lane < 64
    rows = [(c // 2, c % 2 * regs + a, value[c][a]) for c in range(4) for a in range(regs)]
    spot = 0
    for a in plan.tops:
        for c in (0, 2):
            edge = jnp.where(low, value[c][a], roll(value[c + 1][a], 64))
            rows.append((2 + spot // 8, spot % 8, edge))
            spot += 1
    for a in plan.bottoms:
        for c in (0, 2):
            edge = jnp.where(low, roll(value[c][a], 64), value[c + 1][a])
            rows.append((2 + spot // 8, spot % 8, edge))
            spot += 1
    for block, at, row in rows:
        tiles_ref[block, pl.ds(start + at, 8, 8), :] = row


def store_rim(plan, value, tiles_ref, start, column, base):
    lane = lane_of((8, LANES))
    rim = jnp.zeros((8, LANES), jnp.float32)
    for c in range(4):
        for a in range(plan.regs):
            pixels = jnp.where(lane % 64 == column, value[c][a], 0.0)
            rim += roll(pixels, base + 4 * a + c - column)
    block, at = divmod(2 * len(plan.tops) + 2 * len(plan.bottoms), 8)
    tiles_ref[2 + block, pl.ds(start + at, 8, 8), :] = rim


def read_routes(plan, view, route_refs, asked_ref, order_ref):
    for i, route_ref in enumerate(route_refs):
        for r in range(2):
            found = jnp.int32(-1)
            for t in range(plan.columns):
                found = jnp.where(route_ref[r, t] == view, t, found)
            asked_ref[view ^ (2 * i + r)] = found
    asked = [asked_ref[v] for v in range(plan.views)]
    count = jnp.int32(0)
    for t in range(2, plan.columns):
        hit = functools.reduce(jnp.logical_or, [a == t for a in asked])
        order_ref[count + 1] = t
        count = count + jnp.where(hit, 1, 0)
    order_ref[0] = count
    return functools.reduce(jnp.logical_or, [a == 1 for a in asked])


def assemble(plan, tiles_ref, asked_ref, out_ref):
    depths, views, columns = plan.depths, plan.views, plan.columns
    regs, run, band_pairs = plan.regs, plan.run, plan.band
    lane = lane_of((1, LANES))
    zero = jnp.zeros((1, LANES), jnp.float32)
    rim_at = 2 * len(plan.tops) + 2 * len(plan.bottoms)

    def rows_of(block, slot, sublane, at, count):
        return tiles_ref[block, pl.ds(slot * 64 + sublane * 8 + at, count), :]

    asked = [asked_ref[v] for v in range(views)]

    def rim(slot, sublane):
        return rows_of(2 + rim_at // 8, slot, sublane, rim_at % 8, 1)

    def above_of(band):
        sublane, a = plan.run_of(band)
        return (sublane, a - 1) if a > 0 else (sublane - 1, regs - 1)

    def below_of(band):
        sublane, a = plan.run_of(band)
        sublane, a = sublane + (a + band_pairs) // regs, (a + band_pairs) % regs
        return sublane, a

    own, corner = {}, {}
    for slot in (0, columns - 1):
        for band in range(depths):
            sublane, a = plan.run_of(band)
            total = zero
            for i in range(band_pairs // run):
                total = total + roll(rim(slot, sublane + i), 8 * regs * i - 4 * a)
            own[slot, band] = total
            total = zero
            if band > 0:
                sublane, a = above_of(band)
                moved = roll(rim(slot, sublane), 4 * (regs - 1 - a))
                keep = (lane % (4 * regs) >= 4 * (regs - 1)) & (lane >= 64)
                total = total + jnp.where(keep, moved, 0.0)
            if band < depths - 1:
                sublane, a = below_of(band)
                moved = roll(rim(slot, sublane), -4 * a)
                keep = (lane % (4 * regs) < 4) & (lane < 64)
                total = total + jnp.where(keep, moved, 0.0)
            corner[slot, band] = total

    for v in range(views):
        slot = jnp.maximum(asked[v], 0)
        sides = []
        if v + 1 < views:
            sides.append((0, asked[v + 1] == 0))
        if v > 0:
            sides.append((columns - 1, asked[v - 1] == columns - 1))
        for band in range(depths):
            at = plan.peer(band, v) * plan.rows
            first, a = plan.run_of(band)
            for c in range(4):
                for i in range(band_pairs // run):
                    start = at + c * band_pairs + i * run
                    out_ref[pl.ds(start, run), :] = rows_of(
                        c // 2, slot, first + i, c % 2 * regs + a, run
                    )
            at += 4 * band_pairs
            above = below = jnp.zeros((2, LANES), jnp.float32)
            if band > 0:
                sublane, a = above_of(band)
                place = 2 * len(plan.tops) + 2 * plan.bottoms.index(a)
                above = rows_of(2 + place // 8, slot, sublane, place % 8, 2)
            if band < depths - 1:
                sublane, a = below_of(band)
                place = 2 * plan.tops.index(a)
                below = rows_of(2 + place // 8, slot, sublane, place % 8, 2)
            out_ref[pl.ds(at, 2), :] = above
            out_ref[pl.ds(at + 2, 2), :] = below
            out_ref[pl.ds(at + 4, 1), :] = sum(jnp.where(f, own[s, band], 0.0) for s, f in sides) + zero
            mark = jnp.where(lane == LANES - 1, asked[v].astype(jnp.float32), 0.0)
            out_ref[pl.ds(at + 5, 1), :] = sum(jnp.where(f, corner[s, band], 0.0) for s, f in sides) + mark


def fetch(plan, x_ref, slot, held, sems, place, parts):
    size = plan.zts // parts
    return [
        [
            pltpu.make_async_copy(
                x_ref.at[slot, pl.ds(part * size, size), :, a],
                held.at[place, pl.ds(part * size, size), a],
                sems.at[place, part, a],
            )
            for a in range(plan.regs)
        ]
        for part in range(parts)
    ]


def loader(plan, held, place):
    size = plan.zts * plan.regs * 64
    flat = held.reshape(held.shape[0] * size, LANES)

    def load(zt, r, a):
        return flat[pl.ds(place * size + (zt * plan.regs + a) * 64 + r, 8, 8), :]

    return load


def early_kernel(plan, x_ref, pair_ref, tiles_ref, next_ref, held, sems, next_sems):
    parts = fetch(plan, x_ref, 0, held, sems, 0, EARLY_PARTS)
    following = fetch(plan, x_ref, 1, next_ref, next_sems, 0, 1)
    for copies in parts + following:
        for copy in copies:
            copy.start()

    def ready(zt):
        if zt % (plan.zts // EARLY_PARTS) == 0:
            for copy in parts[zt // (plan.zts // EARLY_PARTS)]:
                copy.wait()

    value = march_tile(plan, loader(plan, held, 0), ready)
    store_tile(plan, value, tiles_ref, 0)
    store_rim(plan, value, tiles_ref, 0, 0, 0)
    for copy in following[0]:
        copy.wait()


def late_kernel(plan, view_ref, *refs):
    route_refs, refs = refs[: plan.views // 2], refs[plan.views // 2 :]
    early_ref, next_ref, x_ref, out_ref, tiles_ref, held, sems, early_sem, asked_ref, order_ref = refs
    first = pltpu.make_async_copy(early_ref, tiles_ref.at[:, pl.ds(0, 64)], early_sem)
    first.start()
    second = read_routes(plan, view_ref[0], route_refs, asked_ref, order_ref)
    count = order_ref[0]

    def copies(number):
        slot = order_ref[number + 1]
        return fetch(plan, x_ref, slot, held, sems, number % 2, 1)[0]

    @pl.when(count > 0)
    def _():
        for copy in copies(0):
            copy.start()

    @pl.when(second)
    def _():
        value = march_tile(plan, loader(plan, next_ref, 0))
        store_tile(plan, value, tiles_ref, 64)

    def step(number, carry):
        @pl.when(number + 1 < count)
        def _():
            for copy in copies(number + 1):
                copy.start()

        for copy in copies(number):
            copy.wait()
        value = march_tile(plan, loader(plan, held, number % 2))
        slot = order_ref[number + 1]
        start = pl.multiple_of(slot * 64, 64)
        store_tile(plan, value, tiles_ref, start)

        @pl.when(slot == plan.columns - 1)
        def _():
            store_rim(plan, value, tiles_ref, start, 63, 4 * plan.regs)

        return carry

    lax.fori_loop(0, count, step, 0)
    first.wait()
    assemble(plan, tiles_ref, asked_ref, out_ref)


SMEM = pl.BlockSpec(memory_space=pltpu.SMEM)
VMEM = pl.BlockSpec(memory_space=pltpu.VMEM)
HBM = pl.BlockSpec(memory_space=pltpu.HBM)
ANY = pl.BlockSpec(memory_space=pl.ANY)


def granted(size):
    return pltpu.CompilerParams(vmem_limit_bytes=size)


def cost(plan, bricks):
    samples = bricks * plan.pairs * LANES * STEPS
    return pl.CostEstimate(
        flops=40 * samples, bytes_accessed=6 * samples, transcendentals=5 * samples
    )


def march_early(plan, stored, pair):
    return pl.pallas_call(
        functools.partial(early_kernel, plan),
        in_specs=[HBM, ANY],
        out_specs=[VMEM, VMEM],
        out_shape=[
            jax.ShapeDtypeStruct((plan.blocks, 64, LANES), jnp.float32),
            jax.ShapeDtypeStruct((1, plan.zts, plan.regs, 8, 8, LANES), jnp.float32),
        ],
        scratch_shapes=[
            pltpu.VMEM((1, plan.zts, plan.regs, 8, 8, LANES), jnp.float32),
            pltpu.SemaphoreType.DMA((1, EARLY_PARTS, plan.regs)),
            pltpu.SemaphoreType.DMA((1, 1, plan.regs)),
        ],
        cost_estimate=cost(plan, 1),
        compiler_params=granted(MARCH_BYTES),
        name="march_early",
    )(stored, pair)


def march_late(plan, view, routes, early, following, stored):
    shape = (plan.peers * plan.rows, LANES)
    return pl.pallas_call(
        functools.partial(late_kernel, plan),
        in_specs=[SMEM] + [SMEM] * len(routes) + [ANY, VMEM, HBM],
        out_specs=VMEM,
        out_shape=jax.ShapeDtypeStruct(shape, jnp.float32),
        scratch_shapes=[
            pltpu.VMEM((plan.blocks, plan.columns * 64, LANES), jnp.float32),
            pltpu.VMEM((2, plan.zts, plan.regs, 8, 8, LANES), jnp.float32),
            pltpu.SemaphoreType.DMA((2, 1, plan.regs)),
            pltpu.SemaphoreType.DMA(()),
            pltpu.SMEM((plan.views,), jnp.int32),
            pltpu.SMEM((plan.columns + 1,), jnp.int32),
        ],
        cost_estimate=cost(plan, plan.columns - 1),
        compiler_params=granted(MARCH_BYTES),
        name="march_late",
    )(view, *routes, early, following, stored)


def finish_kernel(plan, source, out_ref, image, marks):
    depths, views, band, columns = plan.depths, plan.views, plan.band, plan.columns
    regs = plan.regs
    lane = lane_of((1, LANES))
    low = lane < 64

    def over(front, alpha, back):
        return front if back is None else front + (1.0 - alpha) * back

    sides = None
    lane2 = lane_of((2, LANES))
    for d in reversed(range(depths)):
        front = None
        for h in range(views):
            n = plan.peer(d, h)
            piece = source[pl.ds(n * plan.rows + 4 * band + 4, 2), :]
            front = piece if front is None else front + piece
            mark = jnp.where(lane == LANES - 1, piece[1:2], 0.0)
            mark = jnp.sum(mark, axis=1, keepdims=True)
            marks[n] = jnp.broadcast_to(mark, (8, LANES))
        alpha = front
        for c in range(3):
            alpha = jnp.where(lane2 % 4 == c, roll(front, c - 3), alpha)
        sides = over(front, alpha, sides)

    bodies, outers = [], []
    low8 = lane_of((8, LANES)) < 64
    even8 = lax.broadcasted_iota(jnp.int32, (8, LANES), 0) % 2 == 0
    for t in range(columns):
        acc, rims = [None] * 4, None
        for d in reversed(range(depths)):
            front = [jnp.zeros((band, LANES), jnp.float32)] * 4
            rim = jnp.zeros((8, LANES), jnp.float32)
            for h in range(views):
                n = plan.peer(d, h)
                at = n * plan.rows
                chosen = marks[n] == t
                front = [
                    jnp.where(chosen[:band], source[pl.ds(at + c * band, band), :], x)
                    for c, x in enumerate(front)
                ]
                rim = jnp.where(chosen, source[pl.ds(at + 4 * band - 2, 8), :], rim)
            acc = [over(f, front[3], b) for f, b in zip(front, acc)]
            alpha = jnp.where(low8, roll(rim, 64), rim)
            alpha = jnp.where(even8, roll(alpha, -1, 0), alpha)
            rims = over(rim, alpha, rims)
        bodies.append(acc)
        outers.append([[rims[2 * side + i + 2 : 2 * side + i + 3] for i in range(2)] for side in range(2)])

    count = 2 * band
    wide = lane_of((band, LANES))
    low_band = wide < 64
    number = lax.broadcasted_iota(jnp.int32, (band, LANES), 0)
    number = 8 * regs * (number // regs) + 4 * (number % regs)
    final = columns // 2 + 1
    spread = jnp.broadcast_to(sides[0:1], (band, LANES))
    for c in range(4):
        for u in range(columns // 2):
            x, y = bodies[2 * u][c], bodies[2 * u + 1][c]
            image[c, u + 1, pl.ds(8, band, 2), :] = jnp.where(low_band, x, roll(y, 64))
            image[c, u + 1, pl.ds(9, band, 2), :] = jnp.where(low_band, roll(x, 64), y)
            for side, at in ((0, 7), (1, 8 + count)):
                x, y = outers[2 * u][side][c // 2], outers[2 * u + 1][side][c // 2]
                if c % 2 == 0:
                    y = roll(y, 64)
                else:
                    x = roll(x, 64)
                image[c, u + 1, pl.ds(at, 1), :] = jnp.where(low, x, y)
        for base, tile, spot in ((0, final, 0), (4 * regs, 0, LANES - 1)):
            for odd in range(2):
                here = wide == base + 64 * odd + number + c
                column = jnp.sum(jnp.where(here, spread, 0.0), axis=1, keepdims=True)
                image[c, tile, pl.ds(8 + odd, band, 2), :] = jnp.where(wide == spot, column, 0.0)
            for at, place in ((7, 64 + base + 4 * (regs - 1) + c), (8 + count, base + c)):
                pixel = jnp.where(lane == place, sides[1:2], 0.0)
                pixel = jnp.sum(pixel, axis=1, keepdims=True)
                image[c, tile, pl.ds(at, 1), :] = jnp.where(lane == spot, pixel, 0.0)

    full = lane_of((count, LANES))
    for c in range(4):
        middle = [image[c, k, pl.ds(8, count), :] for k in range(final + 1)]
        smooth = [
            0.25 * image[c, k, pl.ds(7, count), :]
            + 0.5 * middle[k]
            + 0.25 * image[c, k, pl.ds(9, count), :]
            for k in range(final + 1)
        ]
        later = [roll(x, 1) for x in smooth]
        sooner = [roll(x, -1) for x in smooth]
        for k in range(1, final):
            left = jnp.where(full == 0, later[k - 1], later[k])
            right = jnp.where(full == LANES - 1, sooner[k + 1], sooner[k])
            blurred = 0.25 * left + 0.5 * smooth[k] + 0.25 * right
            out_ref[c, :, pl.ds((k - 1) * LANES, LANES)] = middle[k] + SHARPEN * (
                middle[k] - blurred
            )


def finish(plan, arrived):
    count = 2 * plan.band
    return pl.pallas_call(
        functools.partial(finish_kernel, plan),
        in_specs=[VMEM],
        out_specs=VMEM,
        out_shape=jax.ShapeDtypeStruct((4, count, plan.columns * 64), jnp.float32),
        scratch_shapes=[
            pltpu.VMEM((4, plan.columns // 2 + 2, count + 16, LANES), jnp.float32),
            pltpu.VMEM((plan.peers, 8, LANES), jnp.float32),
        ],
        compiler_params=granted(FINISH_BYTES),
        name="finish",
    )(arrived)


def exchange(plan, messages):
    cut = messages.reshape(plan.peers, plan.rows // 2, 2, LANES)
    moved = lax.all_to_all(cut, PEERS, split_axis=0, concat_axis=0, tiled=True)
    return moved.reshape(plan.peers * plan.rows, LANES)


def swapped(x, distance):
    pairs = [(i, i ^ distance) for i in range(lax.axis_size("view"))]
    return lax.ppermute(x, "view", pairs)


def body(bricks, tile_holder):
    depths, views = lax.axis_size("depth"), lax.axis_size("view")
    columns, edge, area = bricks.shape[2:]
    plan = Plan(depths, views, columns, edge, area)
    view = lax.axis_index("view").astype(jnp.int32).reshape(1)
    own = tile_holder.reshape(1, columns)
    pair = jnp.concatenate([own, swapped(own, 1)], axis=0)
    routes = [pair] + [swapped(pair, k) for k in range(2, views, 2)]
    stored = bricks[0, 0].reshape(columns, plan.zts, 8, plan.pairs, LANES).transpose(0, 1, 3, 2, 4)
    stored = stored.reshape(columns, plan.zts, 8, plan.regs, 8, LANES)
    early, following = march_early(plan, stored, pair)
    messages = march_late(plan, view, routes, early, following, stored)
    return finish(plan, exchange(plan, messages))


def solution(mesh):
    in_specs = (P("depth", "view", None, None, None), P("depth", "view", None))
    out_specs = P(None, "depth", "view")
    return jax.shard_map(body, mesh=mesh, in_specs=in_specs, out_specs=out_specs, check_vma=False)
```

```python
import functools

import jax
import jax.numpy as jnp
from jax import lax
from jax.experimental import pallas as pl
from jax.experimental.pallas import tpu as pltpu
from jax.sharding import PartitionSpec as P

STEPS = 48
DENSITY = 0.8
SHARPEN = 1.5
LANES = 128
PEERS = ("depth", "view")
MARCH_BYTES = 50 * 1024 * 1024
FINISH_BYTES = 16 * 1024 * 1024
EARLY_PARTS = 2


class Plan:
    def __init__(self, depths, views, columns, edge, area):
        self.depths, self.views, self.columns = depths, views, columns
        self.pairs = area // LANES
        self.band = self.pairs // depths
        self.rows = 4 * self.band + 6
        self.peers = depths * views
        self.zts = edge // 8
        self.regs = self.pairs // 8
        self.run = min(self.regs, self.band)
        self.tops = [a for a in range(self.regs) if a % self.band == 0]
        self.bottoms = [a for a in range(self.regs) if (a + 1) % self.run == 0][-len(self.tops) :]
        self.blocks = 3 if len(self.tops) == 1 else 4

    def peer(self, depth, view):
        return depth * self.views + view

    def run_of(self, band):
        pair = band * self.band
        return pair // self.regs, pair % self.regs


def roll(x, shift, axis=1):
    return pltpu.roll(x, shift % x.shape[axis], axis)


def lane_of(shape):
    return lax.broadcasted_iota(jnp.int32, shape, 1)


def march_tile(plan, load, ready=lambda zt: None):
    scale = DENSITY / (2 * STEPS)
    regs = plan.regs
    lane = lane_of((8, LANES))
    row = lax.broadcasted_iota(jnp.int32, (8, LANES), 0)
    low = lane < 64
    inside = (lane % 64 != 0).astype(jnp.float32)
    top, bottom = row == 0, row == 7
    third = 1.0 / 3.0

    def three(zt, part):
        planes = [[load(zt, 4 * part + r, a) for a in range(regs)] for r in range(4)]
        first = [(5.0 * third) * p + third * q for p, q in zip(planes[0], planes[1])]
        second = [p + q for p, q in zip(planes[1], planes[2])]
        last = [third * p + (5.0 * third) * q for p, q in zip(planes[2], planes[3])]
        return [first, second, last]

    def step(index, behind, here, ahead, carry):
        turned = [roll(x, 64) for x in here]
        after = jnp.where(bottom, here[-1], roll(turned[0], -1, 0))
        steps_y = [y - x for x, y in zip(turned, turned[1:] + [after])]
        before = jnp.where(top, turned[0] - here[0], roll(steps_y[-1], 1, 0))
        steps_y = [before] + steps_y
        out = []
        for a in range(regs):
            total, trans, lit, red, blue = carry[a]
            x = here[a]
            grad_y = jnp.where(low, steps_y[a], steps_y[a + 1])
            diff = (x - roll(x, 1)) * inside
            grad_x = diff + roll(diff, -1)
            grad_z = ahead[a] - behind[a]
            norm = grad_x * grad_x + grad_y * grad_y + (grad_z * grad_z + 4.0)
            slope = jnp.abs(grad_z) * lax.rsqrt(norm)
            above = x - 2.0
            total = total + jnp.tanh(above)
            later = jnp.exp(total * -scale - scale * (index + 1))
            part = (trans - later) * (slope + 3.0 / 7.0)
            red = red + part * jnp.tanh(x * 0.375)
            blue = blue + part * jnp.tanh(above * 0.75)
            out.append((total, later, lit + part, red, blue))
        return out

    zero = jnp.zeros((8, LANES), jnp.float32)
    carry = [(zero, zero + 1.0, zero, zero, zero)] * regs
    samples, done = [], 0
    for zt in range(plan.zts):
        ready(zt)
        samples += three(zt, 0) + three(zt, 1)
        if zt == plan.zts - 1:
            samples.append(samples[-1])
        while done + 1 < len(samples):
            carry = step(done, samples[max(done - 1, 0)], *samples[done : done + 2], carry)
            done += 1
    value = [[], [], [], []]
    for _, trans, lit, red, blue in carry:
        value[0].append(0.35 * (lit + red))
        value[1].append(0.35 * (lit - red))
        value[2].append(0.35 * (lit + blue))
        value[3].append(1.0 - trans)
    return value


def store_tile(plan, value, tiles_ref, start):
    regs = plan.regs
    lane = lane_of((8, LANES))
    low = lane < 64
    rows = [(c // 2, c % 2 * regs + a, value[c][a]) for c in range(4) for a in range(regs)]
    spot = 0
    for a in plan.tops:
        for c in (0, 2):
            edge = jnp.where(low, value[c][a], roll(value[c + 1][a], 64))
            rows.append((2 + spot // 8, spot % 8, edge))
            spot += 1
    for a in plan.bottoms:
        for c in (0, 2):
            edge = jnp.where(low, roll(value[c][a], 64), value[c + 1][a])
            rows.append((2 + spot // 8, spot % 8, edge))
            spot += 1
    for block, at, row in rows:
        tiles_ref[block, pl.ds(start + at, 8, 8), :] = row


def store_rim(plan, value, tiles_ref, start, column, base):
    lane = lane_of((8, LANES))
    rim = jnp.zeros((8, LANES), jnp.float32)
    for c in range(4):
        for a in range(plan.regs):
            pixels = jnp.where(lane % 64 == column, value[c][a], 0.0)
            rim += roll(pixels, base + 4 * a + c - column)
    block, at = divmod(2 * len(plan.tops) + 2 * len(plan.bottoms), 8)
    tiles_ref[2 + block, pl.ds(start + at, 8, 8), :] = rim


def read_routes(plan, view, route_refs, asked_ref, order_ref):
    for i, route_ref in enumerate(route_refs):
        for r in range(2):
            found = jnp.int32(-1)
            for t in range(plan.columns):
                found = jnp.where(route_ref[r, t] == view, t, found)
            asked_ref[view ^ (plan.views - 2 - 2 * i + r)] = found
    asked = [asked_ref[v] for v in range(plan.views)]
    count = jnp.int32(0)
    for t in range(3, plan.columns):
        hit = functools.reduce(jnp.logical_or, [a == t for a in asked])
        order_ref[count + 1] = t
        count = count + jnp.where(hit, 1, 0)
    order_ref[0] = count
    return functools.reduce(jnp.logical_or, [a == 2 for a in asked])


def assemble(plan, tiles_ref, asked_ref, out_ref):
    depths, views, columns = plan.depths, plan.views, plan.columns
    regs, run, band_pairs = plan.regs, plan.run, plan.band
    lane = lane_of((1, LANES))
    zero = jnp.zeros((1, LANES), jnp.float32)
    rim_at = 2 * len(plan.tops) + 2 * len(plan.bottoms)

    def rows_of(block, slot, sublane, at, count):
        return tiles_ref[block, pl.ds(slot * 64 + sublane * 8 + at, count), :]

    asked = [asked_ref[v] for v in range(views)]

    def rim(slot, sublane):
        return rows_of(2 + rim_at // 8, slot, sublane, rim_at % 8, 1)

    def above_of(band):
        sublane, a = plan.run_of(band)
        return (sublane, a - 1) if a > 0 else (sublane - 1, regs - 1)

    def below_of(band):
        sublane, a = plan.run_of(band)
        sublane, a = sublane + (a + band_pairs) // regs, (a + band_pairs) % regs
        return sublane, a

    own, corner = {}, {}
    for slot in (0, columns - 1):
        for band in range(depths):
            sublane, a = plan.run_of(band)
            total = zero
            for i in range(band_pairs // run):
                total = total + roll(rim(slot, sublane + i), 8 * regs * i - 4 * a)
            own[slot, band] = total
            total = zero
            if band > 0:
                sublane, a = above_of(band)
                moved = roll(rim(slot, sublane), 4 * (regs - 1 - a))
                keep = (lane % (4 * regs) >= 4 * (regs - 1)) & (lane >= 64)
                total = total + jnp.where(keep, moved, 0.0)
            if band < depths - 1:
                sublane, a = below_of(band)
                moved = roll(rim(slot, sublane), -4 * a)
                keep = (lane % (4 * regs) < 4) & (lane < 64)
                total = total + jnp.where(keep, moved, 0.0)
            corner[slot, band] = total

    for v in range(views):
        slot = jnp.maximum(asked[v], 0)
        sides = []
        if v + 1 < views:
            sides.append((0, asked[v + 1] == 0))
        if v > 0:
            sides.append((columns - 1, asked[v - 1] == columns - 1))
        for band in range(depths):
            at = plan.peer(band, v) * plan.rows
            first, a = plan.run_of(band)
            for c in range(4):
                for i in range(band_pairs // run):
                    start = at + c * band_pairs + i * run
                    out_ref[pl.ds(start, run), :] = rows_of(
                        c // 2, slot, first + i, c % 2 * regs + a, run
                    )
            at += 4 * band_pairs
            above = below = jnp.zeros((2, LANES), jnp.float32)
            if band > 0:
                sublane, a = above_of(band)
                place = 2 * len(plan.tops) + 2 * plan.bottoms.index(a)
                above = rows_of(2 + place // 8, slot, sublane, place % 8, 2)
            if band < depths - 1:
                sublane, a = below_of(band)
                place = 2 * plan.tops.index(a)
                below = rows_of(2 + place // 8, slot, sublane, place % 8, 2)
            out_ref[pl.ds(at, 2), :] = above
            out_ref[pl.ds(at + 2, 2), :] = below
            out_ref[pl.ds(at + 4, 1), :] = sum(jnp.where(f, own[s, band], 0.0) for s, f in sides) + zero
            mark = jnp.where(lane == LANES - 1, asked[v].astype(jnp.float32), 0.0)
            out_ref[pl.ds(at + 5, 1), :] = sum(jnp.where(f, corner[s, band], 0.0) for s, f in sides) + mark


def fetch(plan, x_ref, slot, held, sems, place, parts):
    size = plan.zts // parts
    return [
        [
            pltpu.make_async_copy(
                x_ref.at[slot, pl.ds(part * size, size), :, a],
                held.at[place, pl.ds(part * size, size), a],
                sems.at[place, part, a],
            )
            for a in range(plan.regs)
        ]
        for part in range(parts)
    ]


def loader(plan, held, place):
    size = plan.zts * plan.regs * 64
    flat = held.reshape(held.shape[0] * size, LANES)

    def load(zt, r, a):
        return flat[pl.ds(place * size + (zt * plan.regs + a) * 64 + r, 8, 8), :]

    return load


def first_kernel(plan, x_ref, tiles_ref, next_ref, held, sems, next_sems):
    parts = fetch(plan, x_ref, 0, held, sems, 0, EARLY_PARTS)
    following = fetch(plan, x_ref, 1, next_ref, next_sems, 0, 1)
    for copies in parts + following:
        for copy in copies:
            copy.start()

    def ready(zt):
        if zt % (plan.zts // EARLY_PARTS) == 0:
            for copy in parts[zt // (plan.zts // EARLY_PARTS)]:
                copy.wait()

    value = march_tile(plan, loader(plan, held, 0), ready)
    store_tile(plan, value, tiles_ref, 0)
    store_rim(plan, value, tiles_ref, 0, 0, 0)
    for copy in following[0]:
        copy.wait()


def second_kernel(plan, x_ref, held, pair_ref, tiles_ref, next_ref, next_sems):
    following = fetch(plan, x_ref, 2, next_ref, next_sems, 0, 1)[0]
    for copy in following:
        copy.start()
    store_tile(plan, march_tile(plan, loader(plan, held, 0)), tiles_ref, 0)
    for copy in following:
        copy.wait()


def late_kernel(plan, view_ref, *refs):
    route_refs, refs = refs[: plan.views // 2], refs[plan.views // 2 :]
    early_refs, refs = refs[:2], refs[2:]
    next_ref, x_ref, out_ref, tiles_ref, held, sems, early_sems, asked_ref, order_ref = refs
    ready = [
        pltpu.make_async_copy(ref, tiles_ref.at[:, pl.ds(64 * i, 64)], early_sems.at[i])
        for i, ref in enumerate(early_refs)
    ]
    for copy in ready:
        copy.start()
    third = read_routes(plan, view_ref[0], route_refs, asked_ref, order_ref)
    count = order_ref[0]

    def copies(number):
        slot = order_ref[number + 1]
        return fetch(plan, x_ref, slot, held, sems, number % 2, 1)[0]

    @pl.when(count > 0)
    def _():
        for copy in copies(0):
            copy.start()

    @pl.when(third)
    def _():
        value = march_tile(plan, loader(plan, next_ref, 0))
        store_tile(plan, value, tiles_ref, 128)

    def step(number, carry):
        @pl.when(number + 1 < count)
        def _():
            for copy in copies(number + 1):
                copy.start()

        for copy in copies(number):
            copy.wait()
        value = march_tile(plan, loader(plan, held, number % 2))
        slot = order_ref[number + 1]
        start = pl.multiple_of(slot * 64, 64)
        store_tile(plan, value, tiles_ref, start)

        @pl.when(slot == plan.columns - 1)
        def _():
            store_rim(plan, value, tiles_ref, start, 63, 4 * plan.regs)

        return carry

    lax.fori_loop(0, count, step, 0)
    for copy in ready:
        copy.wait()
    assemble(plan, tiles_ref, asked_ref, out_ref)


SMEM = pl.BlockSpec(memory_space=pltpu.SMEM)
VMEM = pl.BlockSpec(memory_space=pltpu.VMEM)
HBM = pl.BlockSpec(memory_space=pltpu.HBM)
ANY = pl.BlockSpec(memory_space=pl.ANY)


def granted(size):
    return pltpu.CompilerParams(vmem_limit_bytes=size)


def cost(plan, bricks):
    samples = bricks * plan.pairs * LANES * STEPS
    return pl.CostEstimate(
        flops=40 * samples, bytes_accessed=6 * samples, transcendentals=5 * samples
    )


def early_results(plan):
    return dict(
        out_specs=[VMEM, VMEM],
        out_shape=[
            jax.ShapeDtypeStruct((plan.blocks, 64, LANES), jnp.float32),
            jax.ShapeDtypeStruct((1, plan.zts, plan.regs, 8, 8, LANES), jnp.float32),
        ],
        cost_estimate=cost(plan, 1),
        compiler_params=granted(MARCH_BYTES),
    )


def march_first(plan, stored):
    return pl.pallas_call(
        functools.partial(first_kernel, plan),
        in_specs=[HBM],
        scratch_shapes=[
            pltpu.VMEM((1, plan.zts, plan.regs, 8, 8, LANES), jnp.float32),
            pltpu.SemaphoreType.DMA((1, EARLY_PARTS, plan.regs)),
            pltpu.SemaphoreType.DMA((1, 1, plan.regs)),
        ],
        name="march_first",
        **early_results(plan),
    )(stored)


def march_second(plan, stored, fetched, pair):
    return pl.pallas_call(
        functools.partial(second_kernel, plan),
        in_specs=[HBM, VMEM, ANY],
        scratch_shapes=[pltpu.SemaphoreType.DMA((1, 1, plan.regs))],
        name="march_second",
        **early_results(plan),
    )(stored, fetched, pair)


def march_late(plan, view, routes, early, following, stored):
    shape = (plan.peers * plan.rows, LANES)
    return pl.pallas_call(
        functools.partial(late_kernel, plan),
        in_specs=[SMEM] + [SMEM] * len(routes) + [ANY, ANY, VMEM, HBM],
        out_specs=VMEM,
        out_shape=jax.ShapeDtypeStruct(shape, jnp.float32),
        scratch_shapes=[
            pltpu.VMEM((plan.blocks, plan.columns * 64, LANES), jnp.float32),
            pltpu.VMEM((2, plan.zts, plan.regs, 8, 8, LANES), jnp.float32),
            pltpu.SemaphoreType.DMA((2, 1, plan.regs)),
            pltpu.SemaphoreType.DMA((2,)),
            pltpu.SMEM((plan.views,), jnp.int32),
            pltpu.SMEM((plan.columns + 1,), jnp.int32),
        ],
        cost_estimate=cost(plan, plan.columns - 2),
        compiler_params=granted(MARCH_BYTES),
        name="march_late",
    )(view, *routes, *early, following, stored)


def finish_kernel(plan, source, out_ref, image, marks):
    depths, views, band, columns = plan.depths, plan.views, plan.band, plan.columns
    regs = plan.regs
    lane = lane_of((1, LANES))
    low = lane < 64

    def over(front, alpha, back):
        return front if back is None else front + (1.0 - alpha) * back

    sides = None
    lane2 = lane_of((2, LANES))
    for d in reversed(range(depths)):
        front = None
        for h in range(views):
            n = plan.peer(d, h)
            piece = source[pl.ds(n * plan.rows + 4 * band + 4, 2), :]
            front = piece if front is None else front + piece
            mark = jnp.where(lane == LANES - 1, piece[1:2], 0.0)
            mark = jnp.sum(mark, axis=1, keepdims=True)
            marks[n] = jnp.broadcast_to(mark, (8, LANES))
        alpha = front
        for c in range(3):
            alpha = jnp.where(lane2 % 4 == c, roll(front, c - 3), alpha)
        sides = over(front, alpha, sides)

    bodies, outers = [], []
    low8 = lane_of((8, LANES)) < 64
    even8 = lax.broadcasted_iota(jnp.int32, (8, LANES), 0) % 2 == 0
    for t in range(columns):
        acc, rims = [None] * 4, None
        for d in reversed(range(depths)):
            front = [jnp.zeros((band, LANES), jnp.float32)] * 4
            rim = jnp.zeros((8, LANES), jnp.float32)
            for h in range(views):
                n = plan.peer(d, h)
                at = n * plan.rows
                chosen = marks[n] == t
                front = [
                    jnp.where(chosen[:band], source[pl.ds(at + c * band, band), :], x)
                    for c, x in enumerate(front)
                ]
                rim = jnp.where(chosen, source[pl.ds(at + 4 * band - 2, 8), :], rim)
            acc = [over(f, front[3], b) for f, b in zip(front, acc)]
            alpha = jnp.where(low8, roll(rim, 64), rim)
            alpha = jnp.where(even8, roll(alpha, -1, 0), alpha)
            rims = over(rim, alpha, rims)
        bodies.append(acc)
        outers.append([[rims[2 * side + i + 2 : 2 * side + i + 3] for i in range(2)] for side in range(2)])

    count = 2 * band
    wide = lane_of((band, LANES))
    low_band = wide < 64
    number = lax.broadcasted_iota(jnp.int32, (band, LANES), 0)
    number = 8 * regs * (number // regs) + 4 * (number % regs)
    final = columns // 2 + 1
    spread = jnp.broadcast_to(sides[0:1], (band, LANES))
    for c in range(4):
        for u in range(columns // 2):
            x, y = bodies[2 * u][c], bodies[2 * u + 1][c]
            image[c, u + 1, pl.ds(8, band, 2), :] = jnp.where(low_band, x, roll(y, 64))
            image[c, u + 1, pl.ds(9, band, 2), :] = jnp.where(low_band, roll(x, 64), y)
            for side, at in ((0, 7), (1, 8 + count)):
                x, y = outers[2 * u][side][c // 2], outers[2 * u + 1][side][c // 2]
                if c % 2 == 0:
                    y = roll(y, 64)
                else:
                    x = roll(x, 64)
                image[c, u + 1, pl.ds(at, 1), :] = jnp.where(low, x, y)
        for base, tile, spot in ((0, final, 0), (4 * regs, 0, LANES - 1)):
            for odd in range(2):
                here = wide == base + 64 * odd + number + c
                column = jnp.sum(jnp.where(here, spread, 0.0), axis=1, keepdims=True)
                image[c, tile, pl.ds(8 + odd, band, 2), :] = jnp.where(wide == spot, column, 0.0)
            for at, place in ((7, 64 + base + 4 * (regs - 1) + c), (8 + count, base + c)):
                pixel = jnp.where(lane == place, sides[1:2], 0.0)
                pixel = jnp.sum(pixel, axis=1, keepdims=True)
                image[c, tile, pl.ds(at, 1), :] = jnp.where(lane == spot, pixel, 0.0)

    full = lane_of((count, LANES))
    for c in range(4):
        middle = [image[c, k, pl.ds(8, count), :] for k in range(final + 1)]
        smooth = [
            0.25 * image[c, k, pl.ds(7, count), :]
            + 0.5 * middle[k]
            + 0.25 * image[c, k, pl.ds(9, count), :]
            for k in range(final + 1)
        ]
        later = [roll(x, 1) for x in smooth]
        sooner = [roll(x, -1) for x in smooth]
        for k in range(1, final):
            left = jnp.where(full == 0, later[k - 1], later[k])
            right = jnp.where(full == LANES - 1, sooner[k + 1], sooner[k])
            blurred = 0.25 * left + 0.5 * smooth[k] + 0.25 * right
            out_ref[c, :, pl.ds((k - 1) * LANES, LANES)] = middle[k] + SHARPEN * (
                middle[k] - blurred
            )


def finish(plan, arrived):
    count = 2 * plan.band
    return pl.pallas_call(
        functools.partial(finish_kernel, plan),
        in_specs=[VMEM],
        out_specs=VMEM,
        out_shape=jax.ShapeDtypeStruct((4, count, plan.columns * 64), jnp.float32),
        scratch_shapes=[
            pltpu.VMEM((4, plan.columns // 2 + 2, count + 16, LANES), jnp.float32),
            pltpu.VMEM((plan.peers, 8, LANES), jnp.float32),
        ],
        compiler_params=granted(FINISH_BYTES),
        name="finish",
    )(arrived)


def exchange(plan, messages):
    cut = messages.reshape(plan.peers, plan.rows // 2, 2, LANES)
    moved = lax.all_to_all(cut, PEERS, split_axis=0, concat_axis=0, tiled=True)
    return moved.reshape(plan.peers * plan.rows, LANES)


def swapped(x, distance):
    pairs = [(i, i ^ distance) for i in range(lax.axis_size("view"))]
    return lax.ppermute(x, "view", pairs)


def body(bricks, tile_holder):
    depths, views = lax.axis_size("depth"), lax.axis_size("view")
    columns, edge, area = bricks.shape[2:]
    plan = Plan(depths, views, columns, edge, area)
    view = lax.axis_index("view").astype(jnp.int32).reshape(1)
    own = tile_holder.reshape(1, columns)
    pair = jnp.concatenate([own, swapped(own, 1)], axis=0)
    routes = [swapped(pair, k) for k in range(views - 2, 0, -2)] + [pair]
    stored = bricks[0, 0].reshape(columns, plan.zts, 8, plan.pairs, LANES).transpose(0, 1, 3, 2, 4)
    stored = stored.reshape(columns, plan.zts, 8, plan.regs, 8, LANES)
    first, following = march_first(plan, stored)
    second, following = march_second(plan, stored, following, pair)
    messages = march_late(plan, view, routes, (first, second), following, stored)
    return finish(plan, exchange(plan, messages))


def solution(mesh):
    in_specs = (P("depth", "view", None, None, None), P("depth", "view", None))
    out_specs = P(None, "depth", "view")
    return jax.shard_map(body, mesh=mesh, in_specs=in_specs, out_specs=out_specs, check_vma=False)
```

```python
import functools

import jax
import jax.numpy as jnp
from jax import lax
from jax.experimental import pallas as pl
from jax.experimental.pallas import tpu as pltpu
from jax.sharding import PartitionSpec as P

STEPS = 48
DENSITY = 0.8
SHARPEN = 1.5
LANES = 128
PEERS = ("depth", "view")
MARCH_BYTES = 50 * 1024 * 1024
FINISH_BYTES = 16 * 1024 * 1024
EARLY_PARTS = 2


class Plan:
    def __init__(self, depths, views, columns, edge, area):
        self.depths, self.views, self.columns = depths, views, columns
        self.pairs = area // LANES
        self.band = self.pairs // depths
        self.rows = 4 * self.band + 6
        self.peers = depths * views
        self.zts = edge // 8
        self.regs = self.pairs // 8
        self.run = min(self.regs, self.band)
        self.tops = [a for a in range(self.regs) if a % self.band == 0]
        self.bottoms = [a for a in range(self.regs) if (a + 1) % self.run == 0][-len(self.tops) :]
        self.blocks = 3 if len(self.tops) == 1 else 4

    def peer(self, depth, view):
        return depth * self.views + view

    def run_of(self, band):
        pair = band * self.band
        return pair // self.regs, pair % self.regs


def roll(x, shift, axis=1):
    return pltpu.roll(x, shift % x.shape[axis], axis)


def lane_of(shape):
    return lax.broadcasted_iota(jnp.int32, shape, 1)


def march_tile(plan, load, ready=lambda zt: None):
    scale = DENSITY / (2 * STEPS)
    regs = plan.regs
    lane = lane_of((8, LANES))
    row = lax.broadcasted_iota(jnp.int32, (8, LANES), 0)
    low = lane < 64
    inside = (lane % 64 != 0).astype(jnp.float32)
    top, bottom = row == 0, row == 7
    third = 1.0 / 3.0

    def three(zt, part):
        planes = [[load(zt, 4 * part + r, a) for a in range(regs)] for r in range(4)]
        first = [(5.0 * third) * p + third * q for p, q in zip(planes[0], planes[1])]
        second = [p + q for p, q in zip(planes[1], planes[2])]
        last = [third * p + (5.0 * third) * q for p, q in zip(planes[2], planes[3])]
        return [first, second, last]

    def step(index, behind, here, ahead, carry):
        turned = [roll(x, 64) for x in here]
        after = jnp.where(bottom, here[-1], roll(turned[0], -1, 0))
        steps_y = [y - x for x, y in zip(turned, turned[1:] + [after])]
        before = jnp.where(top, turned[0] - here[0], roll(steps_y[-1], 1, 0))
        steps_y = [before] + steps_y
        out = []
        for a in range(regs):
            total, trans, lit, red, blue = carry[a]
            x = here[a]
            grad_y = jnp.where(low, steps_y[a], steps_y[a + 1])
            diff = (x - roll(x, 1)) * inside
            grad_x = diff + roll(diff, -1)
            grad_z = ahead[a] - behind[a]
            norm = grad_x * grad_x + grad_y * grad_y + (grad_z * grad_z + 4.0)
            slope = jnp.abs(grad_z) * lax.rsqrt(norm)
            above = x - 2.0
            total = total + jnp.tanh(above)
            later = jnp.exp(total * -scale - scale * (index + 1))
            part = (trans - later) * (slope + 3.0 / 7.0)
            red = red + part * jnp.tanh(x * 0.375)
            blue = blue + part * jnp.tanh(above * 0.75)
            out.append((total, later, lit + part, red, blue))
        return out

    zero = jnp.zeros((8, LANES), jnp.float32)
    carry = [(zero, zero + 1.0, zero, zero, zero)] * regs
    samples, done = [], 0
    for zt in range(plan.zts):
        ready(zt)
        samples += three(zt, 0) + three(zt, 1)
        if zt == plan.zts - 1:
            samples.append(samples[-1])
        while done + 1 < len(samples):
            carry = step(done, samples[max(done - 1, 0)], *samples[done : done + 2], carry)
            done += 1
    value = [[], [], [], []]
    for _, trans, lit, red, blue in carry:
        value[0].append(0.35 * (lit + red))
        value[1].append(0.35 * (lit - red))
        value[2].append(0.35 * (lit + blue))
        value[3].append(1.0 - trans)
    return value


def store_tile(plan, value, tiles_ref, start):
    regs = plan.regs
    lane = lane_of((8, LANES))
    low = lane < 64
    rows = [(c // 2, c % 2 * regs + a, value[c][a]) for c in range(4) for a in range(regs)]
    spot = 0
    for a in plan.tops:
        for c in (0, 2):
            edge = jnp.where(low, value[c][a], roll(value[c + 1][a], 64))
            rows.append((2 + spot // 8, spot % 8, edge))
            spot += 1
    for a in plan.bottoms:
        for c in (0, 2):
            edge = jnp.where(low, roll(value[c][a], 64), value[c + 1][a])
            rows.append((2 + spot // 8, spot % 8, edge))
            spot += 1
    for block, at, row in rows:
        tiles_ref[block, pl.ds(start + at, 8, 8), :] = row


def store_rim(plan, value, tiles_ref, start, column, base):
    lane = lane_of((8, LANES))
    rim = jnp.zeros((8, LANES), jnp.float32)
    for c in range(4):
        for a in range(plan.regs):
            pixels = jnp.where(lane % 64 == column, value[c][a], 0.0)
            rim += roll(pixels, base + 4 * a + c - column)
    block, at = divmod(2 * len(plan.tops) + 2 * len(plan.bottoms), 8)
    tiles_ref[2 + block, pl.ds(start + at, 8, 8), :] = rim


def read_routes(plan, view, route_refs, asked_ref, order_ref):
    for i, route_ref in enumerate(route_refs):
        for r in range(2):
            found = jnp.int32(-1)
            for t in range(plan.columns):
                found = jnp.where(route_ref[r, t] == view, t, found)
            asked_ref[view ^ (plan.views - 2 - 2 * i + r)] = found
    asked = [asked_ref[v] for v in range(plan.views)]
    count = jnp.int32(0)
    for t in range(3, plan.columns):
        hit = functools.reduce(jnp.logical_or, [a == t for a in asked])
        order_ref[count + 1] = t
        count = count + jnp.where(hit, 1, 0)
    order_ref[0] = count
    return functools.reduce(jnp.logical_or, [a == 2 for a in asked])


def assemble(plan, tiles_ref, asked_ref, out_ref):
    depths, views, columns = plan.depths, plan.views, plan.columns
    regs, run, band_pairs = plan.regs, plan.run, plan.band
    lane = lane_of((1, LANES))
    zero = jnp.zeros((1, LANES), jnp.float32)
    rim_at = 2 * len(plan.tops) + 2 * len(plan.bottoms)

    def rows_of(block, slot, sublane, at, count):
        return tiles_ref[block, pl.ds(slot * 64 + sublane * 8 + at, count), :]

    asked = [asked_ref[v] for v in range(views)]

    def rim(slot, sublane):
        return rows_of(2 + rim_at // 8, slot, sublane, rim_at % 8, 1)

    def above_of(band):
        sublane, a = plan.run_of(band)
        return (sublane, a - 1) if a > 0 else (sublane - 1, regs - 1)

    def below_of(band):
        sublane, a = plan.run_of(band)
        sublane, a = sublane + (a + band_pairs) // regs, (a + band_pairs) % regs
        return sublane, a

    own, corner = {}, {}
    for slot in (0, columns - 1):
        for band in range(depths):
            sublane, a = plan.run_of(band)
            total = zero
            for i in range(band_pairs // run):
                total = total + roll(rim(slot, sublane + i), 8 * regs * i - 4 * a)
            own[slot, band] = total
            total = zero
            if band > 0:
                sublane, a = above_of(band)
                moved = roll(rim(slot, sublane), 4 * (regs - 1 - a))
                keep = (lane % (4 * regs) >= 4 * (regs - 1)) & (lane >= 64)
                total = total + jnp.where(keep, moved, 0.0)
            if band < depths - 1:
                sublane, a = below_of(band)
                moved = roll(rim(slot, sublane), -4 * a)
                keep = (lane % (4 * regs) < 4) & (lane < 64)
                total = total + jnp.where(keep, moved, 0.0)
            corner[slot, band] = total

    for v in range(views):
        slot = jnp.maximum(asked[v], 0)
        sides = []
        if v + 1 < views:
            sides.append((0, asked[v + 1] == 0))
        if v > 0:
            sides.append((columns - 1, asked[v - 1] == columns - 1))
        for band in range(depths):
            at = plan.peer(band, v) * plan.rows
            first, a = plan.run_of(band)
            for c in range(4):
                for i in range(band_pairs // run):
                    start = at + c * band_pairs + i * run
                    out_ref[pl.ds(start, run), :] = rows_of(
                        c // 2, slot, first + i, c % 2 * regs + a, run
                    )
            at += 4 * band_pairs
            above = below = jnp.zeros((2, LANES), jnp.float32)
            if band > 0:
                sublane, a = above_of(band)
                place = 2 * len(plan.tops) + 2 * plan.bottoms.index(a)
                above = rows_of(2 + place // 8, slot, sublane, place % 8, 2)
            if band < depths - 1:
                sublane, a = below_of(band)
                place = 2 * plan.tops.index(a)
                below = rows_of(2 + place // 8, slot, sublane, place % 8, 2)
            out_ref[pl.ds(at, 2), :] = above
            out_ref[pl.ds(at + 2, 2), :] = below
            out_ref[pl.ds(at + 4, 1), :] = sum(jnp.where(f, own[s, band], 0.0) for s, f in sides) + zero
            mark = jnp.where(lane == LANES - 1, asked[v].astype(jnp.float32), 0.0)
            out_ref[pl.ds(at + 5, 1), :] = sum(jnp.where(f, corner[s, band], 0.0) for s, f in sides) + mark


def fetch(plan, x_ref, slot, held, sems, place, parts):
    size = plan.zts // parts
    return [
        [
            pltpu.make_async_copy(
                x_ref.at[slot, pl.ds(part * size, size), :, a],
                held.at[place, pl.ds(part * size, size), a],
                sems.at[place, part, a],
            )
            for a in range(plan.regs)
        ]
        for part in range(parts)
    ]


def loader(plan, held, place):
    size = plan.zts * plan.regs * 64
    flat = held.reshape(held.shape[0] * size, LANES)

    def load(zt, r, a):
        return flat[pl.ds(place * size + (zt * plan.regs + a) * 64 + r, 8, 8), :]

    return load


def first_kernel(plan, x_ref, tiles_ref, next_ref, held, sems, next_sems):
    parts = fetch(plan, x_ref, 0, held, sems, 0, EARLY_PARTS)
    following = fetch(plan, x_ref, 1, next_ref, next_sems, 0, 1)
    for copies in parts + following:
        for copy in copies:
            copy.start()

    def ready(zt):
        if zt % (plan.zts // EARLY_PARTS) == 0:
            for copy in parts[zt // (plan.zts // EARLY_PARTS)]:
                copy.wait()

    value = march_tile(plan, loader(plan, held, 0), ready)
    store_tile(plan, value, tiles_ref, 0)
    store_rim(plan, value, tiles_ref, 0, 0, 0)
    for copy in following[0]:
        copy.wait()


def second_kernel(plan, x_ref, held, pair_ref, tiles_ref, next_ref, next_sems):
    following = fetch(plan, x_ref, 2, next_ref, next_sems, 0, 1)[0]
    for copy in following:
        copy.start()
    store_tile(plan, march_tile(plan, loader(plan, held, 0)), tiles_ref, 0)
    for copy in following:
        copy.wait()


def late_kernel(plan, view_ref, *refs):
    route_refs, refs = refs[: plan.views // 2], refs[plan.views // 2 :]
    early_refs, refs = refs[:2], refs[2:]
    next_ref, x_ref, out_ref, tiles_ref, held, sems, early_sems, asked_ref, order_ref = refs
    ready = [
        pltpu.make_async_copy(ref, tiles_ref.at[:, pl.ds(64 * i, 64)], early_sems.at[i])
        for i, ref in enumerate(early_refs)
    ]
    for copy in ready:
        copy.start()
    third = read_routes(plan, view_ref[0], route_refs, asked_ref, order_ref)
    count = order_ref[0]

    def copies(number):
        slot = order_ref[number + 1]
        return fetch(plan, x_ref, slot, held, sems, number % 2, 1)[0]

    @pl.when(count > 0)
    def _():
        for copy in copies(0):
            copy.start()

    @pl.when(third)
    def _():
        value = march_tile(plan, loader(plan, next_ref, 0))
        store_tile(plan, value, tiles_ref, 128)

    def step(number, carry):
        @pl.when(number + 1 < count)
        def _():
            for copy in copies(number + 1):
                copy.start()

        for copy in copies(number):
            copy.wait()
        value = march_tile(plan, loader(plan, held, number % 2))
        slot = order_ref[number + 1]
        start = pl.multiple_of(slot * 64, 64)
        store_tile(plan, value, tiles_ref, start)

        @pl.when(slot == plan.columns - 1)
        def _():
            store_rim(plan, value, tiles_ref, start, 63, 4 * plan.regs)

        return carry

    lax.fori_loop(0, count, step, 0)
    for copy in ready:
        copy.wait()
    assemble(plan, tiles_ref, asked_ref, out_ref)


SMEM = pl.BlockSpec(memory_space=pltpu.SMEM)
VMEM = pl.BlockSpec(memory_space=pltpu.VMEM)
HBM = pl.BlockSpec(memory_space=pltpu.HBM)
ANY = pl.BlockSpec(memory_space=pl.ANY)


def granted(size):
    return pltpu.CompilerParams(vmem_limit_bytes=size)


def cost(plan, bricks):
    samples = bricks * plan.pairs * LANES * STEPS
    return pl.CostEstimate(
        flops=40 * samples, bytes_accessed=6 * samples, transcendentals=5 * samples
    )


def early_results(plan):
    return dict(
        out_specs=[VMEM, VMEM],
        out_shape=[
            jax.ShapeDtypeStruct((plan.blocks, 64, LANES), jnp.float32),
            jax.ShapeDtypeStruct((1, plan.zts, plan.regs, 8, 8, LANES), jnp.float32),
        ],
        cost_estimate=cost(plan, 1),
        compiler_params=granted(MARCH_BYTES),
    )


def march_first(plan, stored):
    return pl.pallas_call(
        functools.partial(first_kernel, plan),
        in_specs=[HBM],
        scratch_shapes=[
            pltpu.VMEM((1, plan.zts, plan.regs, 8, 8, LANES), jnp.float32),
            pltpu.SemaphoreType.DMA((1, EARLY_PARTS, plan.regs)),
            pltpu.SemaphoreType.DMA((1, 1, plan.regs)),
        ],
        name="march_first",
        **early_results(plan),
    )(stored)


def march_second(plan, stored, fetched, pair):
    return pl.pallas_call(
        functools.partial(second_kernel, plan),
        in_specs=[HBM, VMEM, ANY],
        scratch_shapes=[pltpu.SemaphoreType.DMA((1, 1, plan.regs))],
        name="march_second",
        **early_results(plan),
    )(stored, fetched, pair)


def march_late(plan, view, routes, early, following, stored):
    shape = (plan.peers * plan.rows, LANES)
    return pl.pallas_call(
        functools.partial(late_kernel, plan),
        in_specs=[SMEM] + [SMEM] * len(routes) + [ANY, ANY, VMEM, HBM],
        out_specs=VMEM,
        out_shape=jax.ShapeDtypeStruct(shape, jnp.float32),
        scratch_shapes=[
            pltpu.VMEM((plan.blocks, plan.columns * 64, LANES), jnp.float32),
            pltpu.VMEM((2, plan.zts, plan.regs, 8, 8, LANES), jnp.float32),
            pltpu.SemaphoreType.DMA((2, 1, plan.regs)),
            pltpu.SemaphoreType.DMA((2,)),
            pltpu.SMEM((plan.views,), jnp.int32),
            pltpu.SMEM((plan.columns + 1,), jnp.int32),
        ],
        cost_estimate=cost(plan, plan.columns - 2),
        compiler_params=granted(MARCH_BYTES),
        name="march_late",
    )(view, *routes, *early, following, stored)


def finish_kernel(plan, source, out_ref, image, sender_ref):
    depths, views, band, columns = plan.depths, plan.views, plan.band, plan.columns
    regs = plan.regs
    lane = lane_of((1, LANES))
    low = lane < 64

    def over(front, alpha, back):
        return front if back is None else front + (1.0 - alpha) * back

    for d in range(depths):
        for t in range(columns):
            sender_ref[d, t] = -1
    sides = None
    lane2 = lane_of((2, LANES))
    for d in reversed(range(depths)):
        front = None
        for h in range(views):
            n = plan.peer(d, h)
            piece = source[pl.ds(n * plan.rows + 4 * band + 4, 2), :]
            front = piece if front is None else front + piece
            mark = jnp.where(lane == LANES - 1, piece[1:2], 0.0)
            mark = jnp.sum(mark).astype(jnp.int32)
            sender_ref[d, jnp.where(mark >= 0, mark, columns)] = n
        alpha = front
        for c in range(3):
            alpha = jnp.where(lane2 % 4 == c, roll(front, c - 3), alpha)
        sides = over(front, alpha, sides)

    bodies, outers = [], []
    low8 = lane_of((8, LANES)) < 64
    even8 = lax.broadcasted_iota(jnp.int32, (8, LANES), 0) % 2 == 0
    for t in range(columns):
        acc, rims = [None] * 4, None
        for d in reversed(range(depths)):
            n = sender_ref[d, t]
            at = jnp.maximum(n, 0) * plan.rows
            shown = n >= 0
            front = [
                jnp.where(shown, source[pl.ds(at + c * band, band), :], 0.0) for c in range(4)
            ]
            rim = jnp.where(shown, source[pl.ds(at + 4 * band - 2, 8), :], 0.0)
            acc = [over(f, front[3], b) for f, b in zip(front, acc)]
            alpha = jnp.where(low8, roll(rim, 64), rim)
            alpha = jnp.where(even8, roll(alpha, -1, 0), alpha)
            rims = over(rim, alpha, rims)
        bodies.append(acc)
        outers.append([[rims[2 * side + i + 2 : 2 * side + i + 3] for i in range(2)] for side in range(2)])

    count = 2 * band
    wide = lane_of((band, LANES))
    low_band = wide < 64
    number = lax.broadcasted_iota(jnp.int32, (band, LANES), 0)
    number = 8 * regs * (number // regs) + 4 * (number % regs)
    final = columns // 2 + 1
    spread = jnp.broadcast_to(sides[0:1], (band, LANES))
    for c in range(4):
        for u in range(columns // 2):
            x, y = bodies[2 * u][c], bodies[2 * u + 1][c]
            image[c, u + 1, pl.ds(8, band, 2), :] = jnp.where(low_band, x, roll(y, 64))
            image[c, u + 1, pl.ds(9, band, 2), :] = jnp.where(low_band, roll(x, 64), y)
            for side, at in ((0, 7), (1, 8 + count)):
                x, y = outers[2 * u][side][c // 2], outers[2 * u + 1][side][c // 2]
                if c % 2 == 0:
                    y = roll(y, 64)
                else:
                    x = roll(x, 64)
                image[c, u + 1, pl.ds(at, 1), :] = jnp.where(low, x, y)
        for base, tile, spot in ((0, final, 0), (4 * regs, 0, LANES - 1)):
            for odd in range(2):
                here = wide == base + 64 * odd + number + c
                column = jnp.sum(jnp.where(here, spread, 0.0), axis=1, keepdims=True)
                image[c, tile, pl.ds(8 + odd, band, 2), :] = jnp.where(wide == spot, column, 0.0)
            for at, place in ((7, 64 + base + 4 * (regs - 1) + c), (8 + count, base + c)):
                pixel = jnp.where(lane == place, sides[1:2], 0.0)
                pixel = jnp.sum(pixel, axis=1, keepdims=True)
                image[c, tile, pl.ds(at, 1), :] = jnp.where(lane == spot, pixel, 0.0)

    full = lane_of((count, LANES))
    for c in range(4):
        middle = [image[c, k, pl.ds(8, count), :] for k in range(final + 1)]
        smooth = [
            0.25 * image[c, k, pl.ds(7, count), :]
            + 0.5 * middle[k]
            + 0.25 * image[c, k, pl.ds(9, count), :]
            for k in range(final + 1)
        ]
        later = [roll(x, 1) for x in smooth]
        sooner = [roll(x, -1) for x in smooth]
        for k in range(1, final):
            left = jnp.where(full == 0, later[k - 1], later[k])
            right = jnp.where(full == LANES - 1, sooner[k + 1], sooner[k])
            blurred = 0.25 * left + 0.5 * smooth[k] + 0.25 * right
            out_ref[c, :, pl.ds((k - 1) * LANES, LANES)] = middle[k] + SHARPEN * (
                middle[k] - blurred
            )


def finish(plan, arrived):
    count = 2 * plan.band
    return pl.pallas_call(
        functools.partial(finish_kernel, plan),
        in_specs=[VMEM],
        out_specs=VMEM,
        out_shape=jax.ShapeDtypeStruct((4, count, plan.columns * 64), jnp.float32),
        scratch_shapes=[
            pltpu.VMEM((4, plan.columns // 2 + 2, count + 16, LANES), jnp.float32),
            pltpu.SMEM((plan.depths, plan.columns + 1), jnp.int32),
        ],
        compiler_params=granted(FINISH_BYTES),
        name="finish",
    )(arrived)


def exchange(plan, messages):
    cut = messages.reshape(plan.peers, plan.rows // 2, 2, LANES)
    moved = lax.all_to_all(cut, PEERS, split_axis=0, concat_axis=0, tiled=True)
    return moved.reshape(plan.peers * plan.rows, LANES)


def swapped(x, distance):
    pairs = [(i, i ^ distance) for i in range(lax.axis_size("view"))]
    return lax.ppermute(x, "view", pairs)


def body(bricks, tile_holder):
    depths, views = lax.axis_size("depth"), lax.axis_size("view")
    columns, edge, area = bricks.shape[2:]
    plan = Plan(depths, views, columns, edge, area)
    view = lax.axis_index("view").astype(jnp.int32).reshape(1)
    own = tile_holder.reshape(1, columns)
    pair = jnp.concatenate([own, swapped(own, 1)], axis=0)
    routes = [swapped(pair, k) for k in range(views - 2, 0, -2)] + [pair]
    stored = bricks[0, 0].reshape(columns, plan.zts, 8, plan.pairs, LANES).transpose(0, 1, 3, 2, 4)
    stored = stored.reshape(columns, plan.zts, 8, plan.regs, 8, LANES)
    first, following = march_first(plan, stored)
    second, following = march_second(plan, stored, following, pair)
    messages = march_late(plan, view, routes, (first, second), following, stored)
    return finish(plan, exchange(plan, messages))


def solution(mesh):
    in_specs = (P("depth", "view", None, None, None), P("depth", "view", None))
    out_specs = P(None, "depth", "view")
    return jax.shard_map(body, mesh=mesh, in_specs=in_specs, out_specs=out_specs, check_vma=False)
```

```python
import functools

import jax
import jax.numpy as jnp
from jax import lax
from jax.experimental import pallas as pl
from jax.experimental.pallas import tpu as pltpu
from jax.sharding import PartitionSpec as P

STEPS = 48
DENSITY = 0.8
SHARPEN = 1.5
LANES = 128
PEERS = ("depth", "view")
MARCH_BYTES = 50 * 1024 * 1024
FINISH_BYTES = 16 * 1024 * 1024
EARLY_PARTS = 2


class Plan:
    def __init__(self, depths, views, columns, edge, area):
        self.depths, self.views, self.columns = depths, views, columns
        self.pairs = area // LANES
        self.band = self.pairs // depths
        self.rows = 4 * self.band + 6
        self.peers = depths * views
        self.hops = sorted(range(2, views, 2), key=lambda k: -(k ^ 2))
        self.zts = edge // 8
        self.regs = self.pairs // 8
        self.run = min(self.regs, self.band)
        self.tops = [a for a in range(self.regs) if a % self.band == 0]
        self.bottoms = [a for a in range(self.regs) if (a + 1) % self.run == 0][-len(self.tops) :]
        self.blocks = 3 if len(self.tops) == 1 else 4

    def peer(self, depth, view):
        return depth * self.views + view

    def run_of(self, band):
        pair = band * self.band
        return pair // self.regs, pair % self.regs


def roll(x, shift, axis=1):
    return pltpu.roll(x, shift % x.shape[axis], axis)


def lane_of(shape):
    return lax.broadcasted_iota(jnp.int32, shape, 1)


def march_tile(plan, load, ready=lambda zt: None):
    scale = DENSITY / (2 * STEPS)
    regs = plan.regs
    lane = lane_of((8, LANES))
    row = lax.broadcasted_iota(jnp.int32, (8, LANES), 0)
    low = lane < 64
    inside = (lane % 64 != 0).astype(jnp.float32)
    top, bottom = row == 0, row == 7
    third = 1.0 / 3.0

    def three(zt, part):
        planes = [[load(zt, 4 * part + r, a) for a in range(regs)] for r in range(4)]
        first = [(5.0 * third) * p + third * q for p, q in zip(planes[0], planes[1])]
        second = [p + q for p, q in zip(planes[1], planes[2])]
        last = [third * p + (5.0 * third) * q for p, q in zip(planes[2], planes[3])]
        return [first, second, last]

    def step(index, behind, here, ahead, carry):
        turned = [roll(x, 64) for x in here]
        after = jnp.where(bottom, here[-1], roll(turned[0], -1, 0))
        steps_y = [y - x for x, y in zip(turned, turned[1:] + [after])]
        before = jnp.where(top, turned[0] - here[0], roll(steps_y[-1], 1, 0))
        steps_y = [before] + steps_y
        out = []
        for a in range(regs):
            total, trans, lit, red, blue = carry[a]
            x = here[a]
            grad_y = jnp.where(low, steps_y[a], steps_y[a + 1])
            diff = (x - roll(x, 1)) * inside
            grad_x = diff + roll(diff, -1)
            grad_z = ahead[a] - behind[a]
            norm = grad_x * grad_x + grad_y * grad_y + (grad_z * grad_z + 4.0)
            slope = jnp.abs(grad_z) * lax.rsqrt(norm)
            above = x - 2.0
            total = total + jnp.tanh(above)
            later = jnp.exp(total * -scale - scale * (index + 1))
            part = (trans - later) * (slope + 3.0 / 7.0)
            red = red + part * jnp.tanh(x * 0.375)
            blue = blue + part * jnp.tanh(above * 0.75)
            out.append((total, later, lit + part, red, blue))
        return out

    zero = jnp.zeros((8, LANES), jnp.float32)
    carry = [(zero, zero + 1.0, zero, zero, zero)] * regs
    samples, done = [], 0
    for zt in range(plan.zts):
        ready(zt)
        samples += three(zt, 0) + three(zt, 1)
        if zt == plan.zts - 1:
            samples.append(samples[-1])
        while done + 1 < len(samples):
            carry = step(done, samples[max(done - 1, 0)], *samples[done : done + 2], carry)
            done += 1
    value = [[], [], [], []]
    for _, trans, lit, red, blue in carry:
        value[0].append(0.35 * (lit + red))
        value[1].append(0.35 * (lit - red))
        value[2].append(0.35 * (lit + blue))
        value[3].append(1.0 - trans)
    return value


def store_tile(plan, value, tiles_ref, start):
    regs = plan.regs
    lane = lane_of((8, LANES))
    low = lane < 64
    rows = [(c // 2, c % 2 * regs + a, value[c][a]) for c in range(4) for a in range(regs)]
    spot = 0
    for a in plan.tops:
        for c in (0, 2):
            edge = jnp.where(low, value[c][a], roll(value[c + 1][a], 64))
            rows.append((2 + spot // 8, spot % 8, edge))
            spot += 1
    for a in plan.bottoms:
        for c in (0, 2):
            edge = jnp.where(low, roll(value[c][a], 64), value[c + 1][a])
            rows.append((2 + spot // 8, spot % 8, edge))
            spot += 1
    for block, at, row in rows:
        tiles_ref[block, pl.ds(start + at, 8, 8), :] = row


def store_rim(plan, value, tiles_ref, start, column, base):
    lane = lane_of((8, LANES))
    rim = jnp.zeros((8, LANES), jnp.float32)
    for c in range(4):
        for a in range(plan.regs):
            pixels = jnp.where(lane % 64 == column, value[c][a], 0.0)
            rim += roll(pixels, base + 4 * a + c - column)
    block, at = divmod(2 * len(plan.tops) + 2 * len(plan.bottoms), 8)
    tiles_ref[2 + block, pl.ds(start + at, 8, 8), :] = rim


def read_routes(plan, view, route_refs, asked_ref, order_ref):
    for i, route_ref in enumerate(route_refs):
        for r in range(2):
            found = jnp.int32(-1)
            for t in range(plan.columns):
                found = jnp.where(route_ref[r, t] == view, t, found)
            asked_ref[view ^ ((plan.hops + [0])[i] + r)] = found
    asked = [asked_ref[v] for v in range(plan.views)]
    count = jnp.int32(0)
    for t in range(3, plan.columns):
        hit = functools.reduce(jnp.logical_or, [a == t for a in asked])
        order_ref[count + 1] = t
        count = count + jnp.where(hit, 1, 0)
    order_ref[0] = count
    return functools.reduce(jnp.logical_or, [a == 2 for a in asked])


def assemble(plan, tiles_ref, asked_ref, out_ref):
    depths, views, columns = plan.depths, plan.views, plan.columns
    regs, run, band_pairs = plan.regs, plan.run, plan.band
    lane = lane_of((1, LANES))
    zero = jnp.zeros((1, LANES), jnp.float32)
    rim_at = 2 * len(plan.tops) + 2 * len(plan.bottoms)

    def rows_of(block, slot, sublane, at, count):
        return tiles_ref[block, pl.ds(slot * 64 + sublane * 8 + at, count), :]

    asked = [asked_ref[v] for v in range(views)]

    def rim(slot, sublane):
        return rows_of(2 + rim_at // 8, slot, sublane, rim_at % 8, 1)

    def above_of(band):
        sublane, a = plan.run_of(band)
        return (sublane, a - 1) if a > 0 else (sublane - 1, regs - 1)

    def below_of(band):
        sublane, a = plan.run_of(band)
        sublane, a = sublane + (a + band_pairs) // regs, (a + band_pairs) % regs
        return sublane, a

    own, corner = {}, {}
    for slot in (0, columns - 1):
        for band in range(depths):
            sublane, a = plan.run_of(band)
            total = zero
            for i in range(band_pairs // run):
                total = total + roll(rim(slot, sublane + i), 8 * regs * i - 4 * a)
            own[slot, band] = total
            total = zero
            if band > 0:
                sublane, a = above_of(band)
                moved = roll(rim(slot, sublane), 4 * (regs - 1 - a))
                keep = (lane % (4 * regs) >= 4 * (regs - 1)) & (lane >= 64)
                total = total + jnp.where(keep, moved, 0.0)
            if band < depths - 1:
                sublane, a = below_of(band)
                moved = roll(rim(slot, sublane), -4 * a)
                keep = (lane % (4 * regs) < 4) & (lane < 64)
                total = total + jnp.where(keep, moved, 0.0)
            corner[slot, band] = total

    for v in range(views):
        slot = jnp.maximum(asked[v], 0)
        sides = []
        if v + 1 < views:
            sides.append((0, asked[v + 1] == 0))
        if v > 0:
            sides.append((columns - 1, asked[v - 1] == columns - 1))
        for band in range(depths):
            at = plan.peer(band, v) * plan.rows
            first, a = plan.run_of(band)
            for c in range(4):
                for i in range(band_pairs // run):
                    start = at + c * band_pairs + i * run
                    out_ref[pl.ds(start, run), :] = rows_of(
                        c // 2, slot, first + i, c % 2 * regs + a, run
                    )
            at += 4 * band_pairs
            above = below = jnp.zeros((2, LANES), jnp.float32)
            if band > 0:
                sublane, a = above_of(band)
                place = 2 * len(plan.tops) + 2 * plan.bottoms.index(a)
                above = rows_of(2 + place // 8, slot, sublane, place % 8, 2)
            if band < depths - 1:
                sublane, a = below_of(band)
                place = 2 * plan.tops.index(a)
                below = rows_of(2 + place // 8, slot, sublane, place % 8, 2)
            out_ref[pl.ds(at, 2), :] = above
            out_ref[pl.ds(at + 2, 2), :] = below
            out_ref[pl.ds(at + 4, 1), :] = sum(jnp.where(f, own[s, band], 0.0) for s, f in sides) + zero
            mark = jnp.where(lane == LANES - 1, asked[v].astype(jnp.float32), 0.0)
            out_ref[pl.ds(at + 5, 1), :] = sum(jnp.where(f, corner[s, band], 0.0) for s, f in sides) + mark


def fetch(plan, x_ref, slot, held, sems, place, parts):
    size = plan.zts // parts
    return [
        [
            pltpu.make_async_copy(
                x_ref.at[slot, pl.ds(part * size, size), :, a],
                held.at[place, pl.ds(part * size, size), a],
                sems.at[place, part, a],
            )
            for a in range(plan.regs)
        ]
        for part in range(parts)
    ]


def loader(plan, held, place):
    size = plan.zts * plan.regs * 64
    flat = held.reshape(held.shape[0] * size, LANES)

    def load(zt, r, a):
        return flat[pl.ds(place * size + (zt * plan.regs + a) * 64 + r, 8, 8), :]

    return load


def first_kernel(plan, x_ref, tiles_ref, next_ref, held, sems, next_sems):
    parts = fetch(plan, x_ref, 0, held, sems, 0, EARLY_PARTS)
    following = fetch(plan, x_ref, 1, next_ref, next_sems, 0, 1)
    for copies in parts + following:
        for copy in copies:
            copy.start()

    def ready(zt):
        if zt % (plan.zts // EARLY_PARTS) == 0:
            for copy in parts[zt // (plan.zts // EARLY_PARTS)]:
                copy.wait()

    value = march_tile(plan, loader(plan, held, 0), ready)
    store_tile(plan, value, tiles_ref, 0)
    store_rim(plan, value, tiles_ref, 0, 0, 0)
    for copy in following[0]:
        copy.wait()


def second_kernel(plan, x_ref, held, pair_ref, tiles_ref, next_ref, next_sems):
    following = fetch(plan, x_ref, 2, next_ref, next_sems, 0, 1)[0]
    for copy in following:
        copy.start()
    store_tile(plan, march_tile(plan, loader(plan, held, 0)), tiles_ref, 0)
    for copy in following:
        copy.wait()


def late_kernel(plan, view_ref, *refs):
    route_refs, refs = refs[: plan.views // 2], refs[plan.views // 2 :]
    early_refs, refs = refs[:2], refs[2:]
    next_ref, x_ref, out_ref, tiles_ref, held, sems, early_sems, asked_ref, order_ref = refs
    ready = [
        pltpu.make_async_copy(ref, tiles_ref.at[:, pl.ds(64 * i, 64)], early_sems.at[i])
        for i, ref in enumerate(early_refs)
    ]
    for copy in ready:
        copy.start()
    third = read_routes(plan, view_ref[0], route_refs, asked_ref, order_ref)
    count = order_ref[0]

    def copies(number):
        slot = order_ref[number + 1]
        return fetch(plan, x_ref, slot, held, sems, number % 2, 1)[0]

    @pl.when(count > 0)
    def _():
        for copy in copies(0):
            copy.start()

    @pl.when(third)
    def _():
        value = march_tile(plan, loader(plan, next_ref, 0))
        store_tile(plan, value, tiles_ref, 128)

    def step(number, carry):
        @pl.when(number + 1 < count)
        def _():
            for copy in copies(number + 1):
                copy.start()

        for copy in copies(number):
            copy.wait()
        value = march_tile(plan, loader(plan, held, number % 2))
        slot = order_ref[number + 1]
        start = pl.multiple_of(slot * 64, 64)
        store_tile(plan, value, tiles_ref, start)

        @pl.when(slot == plan.columns - 1)
        def _():
            store_rim(plan, value, tiles_ref, start, 63, 4 * plan.regs)

        return carry

    lax.fori_loop(0, count, step, 0)
    for copy in ready:
        copy.wait()
    assemble(plan, tiles_ref, asked_ref, out_ref)


SMEM = pl.BlockSpec(memory_space=pltpu.SMEM)
VMEM = pl.BlockSpec(memory_space=pltpu.VMEM)
HBM = pl.BlockSpec(memory_space=pltpu.HBM)
ANY = pl.BlockSpec(memory_space=pl.ANY)


def granted(size):
    return pltpu.CompilerParams(vmem_limit_bytes=size)


def cost(plan, bricks):
    samples = bricks * plan.pairs * LANES * STEPS
    return pl.CostEstimate(
        flops=40 * samples, bytes_accessed=6 * samples, transcendentals=5 * samples
    )


def early_results(plan):
    return dict(
        out_specs=[VMEM, VMEM],
        out_shape=[
            jax.ShapeDtypeStruct((plan.blocks, 64, LANES), jnp.float32),
            jax.ShapeDtypeStruct((1, plan.zts, plan.regs, 8, 8, LANES), jnp.float32),
        ],
        cost_estimate=cost(plan, 1),
        compiler_params=granted(MARCH_BYTES),
    )


def march_first(plan, stored):
    return pl.pallas_call(
        functools.partial(first_kernel, plan),
        in_specs=[HBM],
        scratch_shapes=[
            pltpu.VMEM((1, plan.zts, plan.regs, 8, 8, LANES), jnp.float32),
            pltpu.SemaphoreType.DMA((1, EARLY_PARTS, plan.regs)),
            pltpu.SemaphoreType.DMA((1, 1, plan.regs)),
        ],
        name="march_first",
        **early_results(plan),
    )(stored)


def march_second(plan, stored, fetched, pair):
    return pl.pallas_call(
        functools.partial(second_kernel, plan),
        in_specs=[HBM, VMEM, ANY],
        scratch_shapes=[pltpu.SemaphoreType.DMA((1, 1, plan.regs))],
        name="march_second",
        **early_results(plan),
    )(stored, fetched, pair)


def march_late(plan, view, routes, early, following, stored):
    shape = (plan.peers * plan.rows, LANES)
    return pl.pallas_call(
        functools.partial(late_kernel, plan),
        in_specs=[SMEM] + [SMEM] * len(routes) + [ANY, ANY, VMEM, HBM],
        out_specs=VMEM,
        out_shape=jax.ShapeDtypeStruct(shape, jnp.float32),
        scratch_shapes=[
            pltpu.VMEM((plan.blocks, plan.columns * 64, LANES), jnp.float32),
            pltpu.VMEM((2, plan.zts, plan.regs, 8, 8, LANES), jnp.float32),
            pltpu.SemaphoreType.DMA((2, 1, plan.regs)),
            pltpu.SemaphoreType.DMA((2,)),
            pltpu.SMEM((plan.views,), jnp.int32),
            pltpu.SMEM((plan.columns + 1,), jnp.int32),
        ],
        cost_estimate=cost(plan, plan.columns - 2),
        compiler_params=granted(MARCH_BYTES),
        name="march_late",
    )(view, *routes, *early, following, stored)


def finish_kernel(plan, source, out_ref, image, sender_ref):
    depths, views, band, columns = plan.depths, plan.views, plan.band, plan.columns
    regs = plan.regs
    lane = lane_of((1, LANES))
    low = lane < 64

    def over(front, alpha, back):
        return front if back is None else front + (1.0 - alpha) * back

    for d in range(depths):
        for t in range(columns):
            sender_ref[d, t] = -1
    sides = None
    lane2 = lane_of((2, LANES))
    for d in reversed(range(depths)):
        front = None
        for h in range(views):
            n = plan.peer(d, h)
            piece = source[pl.ds(n * plan.rows + 4 * band + 4, 2), :]
            front = piece if front is None else front + piece
            mark = jnp.where(lane == LANES - 1, piece[1:2], 0.0)
            mark = jnp.sum(mark).astype(jnp.int32)
            sender_ref[d, jnp.where(mark >= 0, mark, columns)] = n
        alpha = front
        for c in range(3):
            alpha = jnp.where(lane2 % 4 == c, roll(front, c - 3), alpha)
        sides = over(front, alpha, sides)

    bodies, outers = [], []
    low8 = lane_of((8, LANES)) < 64
    even8 = lax.broadcasted_iota(jnp.int32, (8, LANES), 0) % 2 == 0
    for t in range(columns):
        acc, rims = [None] * 4, None
        for d in reversed(range(depths)):
            n = sender_ref[d, t]
            at = jnp.maximum(n, 0) * plan.rows
            shown = n >= 0
            front = [
                jnp.where(shown, source[pl.ds(at + c * band, band), :], 0.0) for c in range(4)
            ]
            rim = jnp.where(shown, source[pl.ds(at + 4 * band - 2, 8), :], 0.0)
            acc = [over(f, front[3], b) for f, b in zip(front, acc)]
            alpha = jnp.where(low8, roll(rim, 64), rim)
            alpha = jnp.where(even8, roll(alpha, -1, 0), alpha)
            rims = over(rim, alpha, rims)
        bodies.append(acc)
        outers.append([[rims[2 * side + i + 2 : 2 * side + i + 3] for i in range(2)] for side in range(2)])

    count = 2 * band
    wide = lane_of((band, LANES))
    low_band = wide < 64
    number = lax.broadcasted_iota(jnp.int32, (band, LANES), 0)
    number = 8 * regs * (number // regs) + 4 * (number % regs)
    final = columns // 2 + 1
    spread = jnp.broadcast_to(sides[0:1], (band, LANES))
    for c in range(4):
        for u in range(columns // 2):
            x, y = bodies[2 * u][c], bodies[2 * u + 1][c]
            image[c, u + 1, pl.ds(8, band, 2), :] = jnp.where(low_band, x, roll(y, 64))
            image[c, u + 1, pl.ds(9, band, 2), :] = jnp.where(low_band, roll(x, 64), y)
            for side, at in ((0, 7), (1, 8 + count)):
                x, y = outers[2 * u][side][c // 2], outers[2 * u + 1][side][c // 2]
                if c % 2 == 0:
                    y = roll(y, 64)
                else:
                    x = roll(x, 64)
                image[c, u + 1, pl.ds(at, 1), :] = jnp.where(low, x, y)
        for base, tile, spot in ((0, final, 0), (4 * regs, 0, LANES - 1)):
            for odd in range(2):
                here = wide == base + 64 * odd + number + c
                column = jnp.sum(jnp.where(here, spread, 0.0), axis=1, keepdims=True)
                image[c, tile, pl.ds(8 + odd, band, 2), :] = jnp.where(wide == spot, column, 0.0)
            for at, place in ((7, 64 + base + 4 * (regs - 1) + c), (8 + count, base + c)):
                pixel = jnp.where(lane == place, sides[1:2], 0.0)
                pixel = jnp.sum(pixel, axis=1, keepdims=True)
                image[c, tile, pl.ds(at, 1), :] = jnp.where(lane == spot, pixel, 0.0)

    full = lane_of((count, LANES))
    for c in range(4):
        middle = [image[c, k, pl.ds(8, count), :] for k in range(final + 1)]
        smooth = [
            0.25 * image[c, k, pl.ds(7, count), :]
            + 0.5 * middle[k]
            + 0.25 * image[c, k, pl.ds(9, count), :]
            for k in range(final + 1)
        ]
        later = [roll(x, 1) for x in smooth]
        sooner = [roll(x, -1) for x in smooth]
        for k in range(1, final):
            left = jnp.where(full == 0, later[k - 1], later[k])
            right = jnp.where(full == LANES - 1, sooner[k + 1], sooner[k])
            blurred = 0.25 * left + 0.5 * smooth[k] + 0.25 * right
            out_ref[c, :, pl.ds((k - 1) * LANES, LANES)] = middle[k] + SHARPEN * (
                middle[k] - blurred
            )


def finish(plan, arrived):
    count = 2 * plan.band
    return pl.pallas_call(
        functools.partial(finish_kernel, plan),
        in_specs=[VMEM],
        out_specs=VMEM,
        out_shape=jax.ShapeDtypeStruct((4, count, plan.columns * 64), jnp.float32),
        scratch_shapes=[
            pltpu.VMEM((4, plan.columns // 2 + 2, count + 16, LANES), jnp.float32),
            pltpu.SMEM((plan.depths, plan.columns + 1), jnp.int32),
        ],
        compiler_params=granted(FINISH_BYTES),
        name="finish",
    )(arrived)


def exchange(plan, messages):
    cut = messages.reshape(plan.peers, plan.rows // 2, 2, LANES)
    moved = lax.all_to_all(cut, PEERS, split_axis=0, concat_axis=0, tiled=True)
    return moved.reshape(plan.peers * plan.rows, LANES)


def swapped(x, distance):
    pairs = [(i, i ^ distance) for i in range(lax.axis_size("view"))]
    return lax.ppermute(x, "view", pairs)


def body(bricks, tile_holder):
    depths, views = lax.axis_size("depth"), lax.axis_size("view")
    columns, edge, area = bricks.shape[2:]
    plan = Plan(depths, views, columns, edge, area)
    view = lax.axis_index("view").astype(jnp.int32).reshape(1)
    own = tile_holder.reshape(1, columns)
    pair = jnp.concatenate([own, swapped(own, 1)], axis=0)
    routes = [swapped(pair, k) for k in plan.hops] + [pair]
    stored = bricks[0, 0].reshape(columns, plan.zts, 8, plan.pairs, LANES).transpose(0, 1, 3, 2, 4)
    stored = stored.reshape(columns, plan.zts, 8, plan.regs, 8, LANES)
    first, following = march_first(plan, stored)
    second, following = march_second(plan, stored, following, pair)
    messages = march_late(plan, view, routes, (first, second), following, stored)
    return finish(plan, exchange(plan, messages))


def solution(mesh):
    in_specs = (P("depth", "view", None, None, None), P("depth", "view", None))
    out_specs = P(None, "depth", "view")
    return jax.shard_map(body, mesh=mesh, in_specs=in_specs, out_specs=out_specs, check_vma=False)
```
